32 devices in a mesh: tm: 16 (over z, y, core), row: 2 (over x).
Axes of the slice: x: 2, y: 2, z: 4, core: 2. Of those that a mesh axis runs over, the one named last changes fastest.
Arguments:
- wavefront: float32 [128, 2, 256, 256], P('tm', None, 'row'), may hold values from -6 to 6
- particle_phase: float32 [128, 4096], P('tm', 'row'), may hold values from -3.140625 to 3.140625
- particle_energy: float32 [128, 4096], P('tm', 'row'), may hold values from -6 to 6
- row_offset: float32 [128, 4096], P('tm', 'row'), may hold values from -0.5 to 0.5
- row_cell: int32 [128, 4096], P('tm', 'row'), may hold values from 0 to 255, as said below
- col_cell: int32 [128, 4096], P('tm', 'row'), may hold values from 0 to 255
Outputs:
- wavefront_out: float32 [128, 2, 256, 256], P('tm', None, 'row')
- phase_out: float32 [128, 4096], P('tm', 'row')
- energy_out: float32 [128, 4096], P('tm', 'row')
The draws below stay inside these ranges and needn't reach their ends.
Inputs may be any that keep to these rules, and one draw needn't show every extreme that they name: `row_cell`: the particle at position p of a slice lies in rows 128 * (p // 2048) to 128 * (p // 2048) + 127.
All inputs are finite; a program needn't handle non-finite values.
Results may differ from the reference program's by a relative error of at most 0.0003.
Values sent between devices are 32-bit elements; how exact they have to be, the bound alone decides.
A program may use at most 64 MiB of HBM per device.

```python
import math
import jax
import jax.numpy as jnp
from jax import lax

NR = 256
NC = 256
P_SIZE = 4096
STEPS = 2
SLICES = 128
ROWS_DEV = 128
PART_DEV = 2048


def draw_row_cell(key, part):
    position = jnp.arange(P_SIZE, dtype=jnp.int32)[None, :]
    inside = jax.random.randint(key, (SLICES, P_SIZE), 0, ROWS_DEV, dtype=jnp.int32)
    within = position % PART_DEV
    inside = jnp.where(within == 0, 0, jnp.where(within == 1, ROWS_DEV - 1, inside))
    return position // PART_DEV * ROWS_DEV + inside


def plant(array, stream_key, low, top_value):
    shape = array.shape
    place = [jax.random.randint(jax.random.fold_in(stream_key, axis), (), 0, shape[axis]) for axis in range(len(shape))]
    array = array.at[tuple(place)].set(low)
    longest = shape.index(max(shape))
    place[longest] = (place[longest] + 1) % shape[longest]
    return array.at[tuple(place)].set(top_value)


def block_scale(stream_key, shape, pieces, least, top_value):
    def one(dim, blocks):
        draws = jax.random.uniform(jax.random.fold_in(jax.random.fold_in(stream_key, 6), dim), (blocks,), jnp.float32, least / len(pieces), top_value / len(pieces))
        return jnp.repeat(jnp.exp(draws), shape[dim] // blocks).reshape((-1,) + (1,) * (len(shape) - dim - 1))

    gain = one(*pieces[0])
    for cut in pieces[1:]:
        gain = gain * one(*cut)
    return gain


def scatter_about(own_key, shape, deviation, limit, cuts=(), held_as=jnp.bfloat16):
    array = jax.random.normal(own_key, shape, jnp.float32) * deviation
    if len(cuts) > 0:
        array = block_scale(own_key, shape, cuts, -0.22, 0.18) * array
    return jnp.clip(array, min=-limit, max=limit).astype(held_as)


def setup_inputs(seed: int = 0) -> dict:
    splits = jax.random.split(jax.random.key(seed), 7)
    return {
        "wavefront": scatter_about(splits[0], (SLICES, 2, NR, NC), 1.0, 6.0, ((0, 16), (2, 2)), jnp.float32),
        "particle_phase": jnp.clip(jax.random.uniform(splits[1], (SLICES, P_SIZE), jnp.float32, -3.140625, 3.140625), -3.140625, 3.140625),
        "particle_energy": scatter_about(splits[2], (SLICES, P_SIZE), 1.0, 6.0, ((0, 16), (1, 2)), jnp.float32),
        "row_offset": jnp.clip(jax.random.uniform(splits[3], (SLICES, P_SIZE), jnp.float32, -0.5, 0.5) * block_scale(splits[3], (SLICES, P_SIZE), ((0, 16), (1, 2)), -0.4, 0.0), -0.5, 0.5),
        "row_cell": draw_row_cell(jax.random.fold_in(splits[6], 71), 0),
        "col_cell": plant(jax.random.randint(splits[5], (SLICES, P_SIZE), 0, NC), jax.random.fold_in(splits[5], 1), 0, NC - 1).astype(jnp.int32),
    }


PUSH_GAIN = 0.5
PHASE_ADVANCE = 1.0
SOURCE_GAIN = 1.0


def phase_ramp(length):
    number = jnp.arange(length, dtype=jnp.int32)
    signed = jnp.where(number < length // 2, number, number - length).astype(jnp.float32)
    return (math.pi / length) * signed * signed


def interact(wavefront, padded, halo_rows, own_rows, col_cell, particle_phase, particle_energy, row_offset):
    slice_count = padded.shape[0]
    col_total = padded.shape[3]
    flattened = padded.reshape(slice_count, 2, padded.shape[2] * col_total)

    def sample_at(row_shift):
        target = (halo_rows + row_shift) * col_total + col_cell
        return (jnp.take_along_axis(flattened[:, 0], target, axis=1),
                jnp.take_along_axis(flattened[:, 1], target, axis=1))

    low_real, low_imag = sample_at(-1)
    mid_real, mid_imag = sample_at(0)
    high_real, high_imag = sample_at(1)
    lower_gap = 0.5 - row_offset
    upper_gap = 0.5 + row_offset
    weight_low = 0.5 * lower_gap * lower_gap
    weight_mid = 0.75 - row_offset * row_offset
    weight_high = 0.5 * upper_gap * upper_gap
    sampled_real = weight_low * low_real + weight_mid * mid_real + weight_high * high_real
    sampled_imag = weight_low * low_imag + weight_mid * mid_imag + weight_high * high_imag
    driving = sampled_real * jnp.cos(particle_phase) - sampled_imag * jnp.sin(particle_phase)
    particle_energy = particle_energy - PUSH_GAIN * driving
    particle_phase = particle_phase + PHASE_ADVANCE * particle_energy
    rows_own = wavefront.shape[2]
    target = own_rows * col_total + col_cell
    slice_index = jnp.arange(slice_count, dtype=jnp.int32)[:, None]
    deposit = jnp.zeros((slice_count, 2, rows_own * col_total), jnp.float32)
    deposit = deposit.at[slice_index, 0, target].add(SOURCE_GAIN * jnp.cos(particle_phase))
    deposit = deposit.at[slice_index, 1, target].add(-SOURCE_GAIN * jnp.sin(particle_phase))
    return wavefront + deposit.reshape(wavefront.shape), particle_phase, particle_energy


def reference(wavefront, particle_phase, particle_energy, row_offset, row_cell, col_cell):
    total_phase = phase_ramp(NR)[:, None] + phase_ramp(NC)[None, :]
    factor = lax.complex(jnp.cos(total_phase), -jnp.sin(total_phase))
    for period in range(STEPS):
        wavefront = jnp.concatenate([jnp.zeros_like(wavefront[:1]), wavefront[:-1]], 0)
        padded = jnp.pad(wavefront, ((0, 0), (0, 0), (1, 1), (0, 0)))
        wavefront, particle_phase, particle_energy = interact(
            wavefront, padded, row_cell + 1, row_cell, col_cell,
            particle_phase, particle_energy, row_offset)
        complex_wave = lax.complex(wavefront[:, 0], wavefront[:, 1])
        complex_wave = jnp.fft.ifft2(jnp.fft.fft2(complex_wave) * factor)
        wavefront = jnp.stack([jnp.real(complex_wave), jnp.imag(complex_wave)], 1)
    return wavefront, particle_phase, particle_energy
```

```python
import math

import jax
import jax.numpy as jnp
import ml_dtypes
import numpy as np
from jax import lax
from jax.experimental import pallas as pl
from jax.experimental.pallas import tpu as pltpu
from jax.sharding import PartitionSpec as P

PUSH_GAIN = 0.5
PHASE_ADVANCE = 1.0
SOURCE_GAIN = 1.0
LANES = 512
BF16 = jnp.bfloat16
F32 = jnp.float32


def diffraction_matrix(length):
    number = np.arange(length)
    signed = np.where(number < length // 2, number, number - length).astype(np.float64)
    kernel = np.fft.ifft(np.exp(-1j * math.pi / length * signed * signed))
    return kernel[(number[:, None] - number[None, :]) % length]


def two_parts(matrix):
    high = matrix.astype(ml_dtypes.bfloat16)
    low = (matrix - high.astype(np.float64)).astype(ml_dtypes.bfloat16)
    return high, low


def split(value):
    high = value.astype(BF16)
    return high, (value - high.astype(F32)).astype(BF16)


def sine_cosine(angle):
    count = jnp.round(angle * (2.0 / math.pi))
    rest = angle - count * 1.5703125
    rest = rest - count * 4.837512969970703125e-4
    rest = rest - count * 7.54978995489188216e-8
    quadrant = count.astype(jnp.int32)
    square = rest * rest
    sine = rest + rest * square * (
        -1.6666654611e-1 + square * (8.3321608736e-3 + square * -1.9515295891e-4)
    )
    cosine = 1.0 + square * (
        -0.5 + square * (4.166664568298827e-2 + square * (-1.388731625493765e-3 + square * 2.443315711809948e-5))
    )
    swapped = (quadrant & 1) == 1
    sine_out = jnp.where(swapped, cosine, sine)
    cosine_out = jnp.where(swapped, sine, cosine)
    sine_out = jnp.where((quadrant & 2) == 2, -sine_out, sine_out)
    cosine_out = jnp.where(((quadrant + 1) & 2) == 2, -cosine_out, cosine_out)
    return sine_out, cosine_out


def dot(left, right):
    return jnp.dot(left, right, preferred_element_type=F32)


def push(field, row, col, offset, phase, energy, hot, sampled):
    rows, cols = field.shape[1], field.shape[2]
    half_rows = rows // 2
    window = half_rows + 16
    groups = row.shape[0] // 2
    lanes = row.shape[1]
    cells = lax.broadcasted_iota(jnp.int32, (cols, lanes), 0)
    for half in range(2):
        start = 0 if half == 0 else half_rows - 16
        high, low = split(field[:, pl.ds(start, window), :].reshape(2 * window, cols))
        row_ids = lax.broadcasted_iota(jnp.int32, (window, lanes), 0) + start
        for group in range(groups):
            at = half * groups + group
            here = pl.ds(at, 1)
            one_hot = jnp.where(cells == col[here, :], 1.0, 0.0).astype(BF16)
            hot[:, pl.ds(at * lanes, lanes)] = one_hot
            mixed = dot(high, one_hot) + dot(low, one_hot)
            away = row_ids - row[here, :]
            f = offset[here, :]
            weight = jnp.where(away == -1, 0.5 * (0.5 - f) * (0.5 - f), 0.0)
            weight = jnp.where(away == 0, 0.75 - f * f, weight)
            weight = jnp.where(away == 1, 0.5 * (0.5 + f) * (0.5 + f), weight)
            sampled[0, here, :] = jnp.sum(weight * mixed[:window], axis=0, keepdims=True)
            sampled[1, here, :] = jnp.sum(weight * mixed[window:], axis=0, keepdims=True)
    sine, cosine = sine_cosine(phase)
    energy = energy - PUSH_GAIN * (sampled[0] * cosine - sampled[1] * sine)
    return phase + PHASE_ADVANCE * energy, energy


def deposit(field, row, phase, hot, source):
    rows = field.shape[1]
    half_rows = rows // 2
    groups = row.shape[0] // 2
    lanes = row.shape[1]
    sine, cosine = sine_cosine(phase)
    source[0] = SOURCE_GAIN * cosine
    source[1] = -SOURCE_GAIN * sine
    for half in range(2):
        row_ids = lax.broadcasted_iota(jnp.int32, (half_rows, lanes), 0) + half * half_rows
        total = None
        for group in range(groups):
            at = half * groups + group
            here = pl.ds(at, 1)
            match = row_ids == row[here, :]
            parts = []
            for part in range(2):
                high, low = split(jnp.where(match, source[part, here, :], 0.0))
                parts += [high, low]
            term = lax.dot_general(
                jnp.concatenate(parts, 0),
                hot[:, pl.ds(at * lanes, lanes)],
                (((1,), (1,)), ((), ())),
                preferred_element_type=F32,
            )
            total = term if total is None else total + term
        own = pl.ds(half * half_rows, half_rows)
        for part in range(2):
            first = total[2 * part * half_rows : (2 * part + 1) * half_rows]
            second = total[(2 * part + 1) * half_rows : (2 * part + 2) * half_rows]
            field[part, own, :] += first + second


def diffract(field, out, mat):
    rows, cols = field.shape[1], field.shape[2]
    mat_high, mat_low = mat[0], mat[1]
    wide_high = jnp.concatenate([mat_high[:cols], mat_high[cols:]], 1)
    wide_low = jnp.concatenate([mat_low[:cols], mat_low[cols:]], 1)
    high, low = split(field[...].reshape(2 * rows, cols))
    turned = dot(high, wide_high) + dot(high, wide_low) + dot(low, wide_high)
    real = turned[:rows, :cols] - turned[rows:, cols:]
    imag = turned[:rows, cols:] + turned[rows:, :cols]
    high, low = split(jnp.concatenate([real, imag], 1))
    turned = dot(mat_high, high) + dot(mat_high, low) + dot(mat_low, high)
    out[0] = turned[:rows, :cols] - turned[rows:, cols:]
    out[1] = turned[:rows, cols:] + turned[rows:, :cols]


def step_kernel(field, row, col, offset, phase, energy, mat, out, phase_out, energy_out, hot, work, sampled, source):
    @pl.loop(0, field.shape[0])
    def _(slot):
        work[...] = field[slot]
        new_phase, new_energy = push(
            work, row.at[slot], col.at[slot], offset.at[slot], phase[slot], energy[slot], hot, sampled
        )
        phase_out[slot] = new_phase
        energy_out[slot] = new_energy
        deposit(work, row.at[slot], new_phase, hot, source)
        diffract(work, out.at[slot], mat)


def step(field, cells, mat):
    slots, _, rows, cols = field.shape
    particles = cells[0].shape
    vmem = pl.BlockSpec(memory_space=pltpu.VMEM)
    return pl.pallas_call(
        step_kernel,
        out_shape=(
            jax.ShapeDtypeStruct(field.shape, F32),
            jax.ShapeDtypeStruct(particles, F32),
            jax.ShapeDtypeStruct(particles, F32),
        ),
        in_specs=[vmem] * 7,
        out_specs=(vmem,) * 3,
        scratch_shapes=[
            pltpu.VMEM((cols, particles[1] * particles[2]), BF16),
            pltpu.VMEM((2, rows, cols), F32),
            pltpu.VMEM((2,) + particles[1:], F32),
            pltpu.VMEM((2,) + particles[1:], F32),
        ],
        compiler_params=pltpu.CompilerParams(vmem_limit_bytes=48 * 1024 * 1024),
        cost_estimate=pl.CostEstimate(flops=20 * 10**9, bytes_accessed=4 * 2**20, transcendentals=0),
    )(field, *cells, mat)


def body(wavefront, particle_phase, particle_energy, row_offset, row_cell, col_cell):
    blocks, halves = lax.axis_size("tm"), lax.axis_size("row")
    count = blocks * halves
    me = lax.axis_index("tm") * halves + lax.axis_index("row")
    axes = ("tm", "row")
    incoming = lax.ppermute(wavefront[-1:], "tm", [(i, i + 1) for i in range(blocks - 1)])
    field = jnp.concatenate([incoming, wavefront[:-1]], 0)
    field = lax.all_to_all(field, "row", split_axis=0, concat_axis=2, tiled=True)
    rows, cols = field.shape[2], field.shape[3]
    matrix = diffraction_matrix(cols)
    mat = jnp.asarray(np.stack(two_parts(np.concatenate([matrix.real, matrix.imag], 0))))
    whole = jnp.stack([particle_phase, particle_energy, row_offset, row_cell.astype(F32), col_cell.astype(F32)])
    whole = lax.all_to_all(whole, "row", split_axis=1, concat_axis=2, tiled=True)
    whole = whole.reshape(5, whole.shape[1], -1, LANES)

    def cells(data):
        return (data[3].astype(jnp.int32), data[4].astype(jnp.int32), data[2], data[0], data[1])

    field, phase, energy = step(field, cells(whole), mat)
    whole = jnp.concatenate([phase[None], energy[None], whole[2:]], 0)
    ahead = lax.ppermute(whole[:, :1], axes, [(i, (i - 1) % count) for i in range(count)])
    whole = jnp.concatenate([whole[:, 1:], ahead], 1)
    keep = jnp.where(me == count - 1, 0.0, 1.0)
    field = jnp.concatenate([field[:-1], jnp.where(keep == 0.0, 0.0, field[-1:])], 0)
    field, phase, energy = step(field, cells(whole), mat)
    forward = [(i, (i + 1) % count) for i in range(count)]
    field = jnp.concatenate([lax.ppermute(field[-1:], axes, forward), field[:-1]], 0)
    pair = jnp.stack([phase, energy]).reshape(2, phase.shape[0], -1)
    pair = jnp.concatenate([lax.ppermute(pair[:, -1:], axes, forward), pair[:, :-1]], 1)
    field = lax.all_to_all(field, "row", split_axis=2, concat_axis=0, tiled=True)
    pair = lax.all_to_all(pair, "row", split_axis=2, concat_axis=1, tiled=True)
    return field, pair[0], pair[1]


def solution(mesh):
    specs = (P("tm", None, "row", None),) + (P("tm", "row"),) * 5
    return jax.shard_map(body, mesh=mesh, in_specs=specs, out_specs=specs[:3], check_vma=False)
```

```python
import functools
import math

import jax
import jax.numpy as jnp
import ml_dtypes
import numpy as np
from jax import lax
from jax.experimental import pallas as pl
from jax.experimental.pallas import tpu as pltpu
from jax.sharding import PartitionSpec as P

PUSH_GAIN = 0.5
PHASE_ADVANCE = 1.0
SOURCE_GAIN = 1.0
LANES = 512
BF16 = jnp.bfloat16
F32 = jnp.float32


def diffraction_matrix(length):
    number = np.arange(length)
    signed = np.where(number < length // 2, number, number - length).astype(np.float64)
    kernel = np.fft.ifft(np.exp(-1j * math.pi / length * signed * signed))
    return kernel[(number[:, None] - number[None, :]) % length]


def two_parts(matrix):
    high = matrix.astype(ml_dtypes.bfloat16)
    low = (matrix - high.astype(np.float64)).astype(ml_dtypes.bfloat16)
    return high, low


def split(value):
    high = value.astype(BF16)
    return high, (value - high.astype(F32)).astype(BF16)


def sine_cosine(angle):
    count = jnp.round(angle * (2.0 / math.pi))
    rest = angle - count * 1.5703125
    rest = rest - count * 4.837512969970703125e-4
    rest = rest - count * 7.54978995489188216e-8
    quadrant = count.astype(jnp.int32)
    square = rest * rest
    sine = rest + rest * square * (
        -1.6666654611e-1 + square * (8.3321608736e-3 + square * -1.9515295891e-4)
    )
    cosine = 1.0 + square * (
        -0.5 + square * (4.166664568298827e-2 + square * (-1.388731625493765e-3 + square * 2.443315711809948e-5))
    )
    swapped = (quadrant & 1) == 1
    sine_out = jnp.where(swapped, cosine, sine)
    cosine_out = jnp.where(swapped, sine, cosine)
    sine_out = jnp.where((quadrant & 2) == 2, -sine_out, sine_out)
    cosine_out = jnp.where(((quadrant + 1) & 2) == 2, -cosine_out, cosine_out)
    return sine_out, cosine_out


def dot(left, right):
    return jnp.dot(left, right, preferred_element_type=F32)


def push(field, cell, hot, sampled):
    phase, energy, offset, row, col = (cell.at[item] for item in range(5))
    rows, cols = field.shape[1], field.shape[2]
    half_rows = rows // 2
    window = half_rows + 16
    groups = row.shape[0] // 2
    lanes = row.shape[1]
    cells = lax.broadcasted_iota(jnp.int32, (cols, lanes), 0).astype(F32)
    for half in range(2):
        start = 0 if half == 0 else half_rows - 16
        high, low = split(field[:, pl.ds(start, window), :].reshape(2 * window, cols))
        row_ids = (lax.broadcasted_iota(jnp.int32, (window, lanes), 0) + start).astype(F32)
        for group in range(groups):
            at = half * groups + group
            here = pl.ds(at, 1)
            one_hot = jnp.where(cells == col[here, :], 1.0, 0.0).astype(BF16)
            hot[:, pl.ds(at * lanes, lanes)] = one_hot
            mixed = dot(high, one_hot) + dot(low, one_hot)
            away = row_ids - row[here, :]
            f = offset[here, :]
            weight = jnp.where(away == -1, 0.5 * (0.5 - f) * (0.5 - f), 0.0)
            weight = jnp.where(away == 0, 0.75 - f * f, weight)
            weight = jnp.where(away == 1, 0.5 * (0.5 + f) * (0.5 + f), weight)
            sampled[0, here, :] = jnp.sum(weight * mixed[:window], axis=0, keepdims=True)
            sampled[1, here, :] = jnp.sum(weight * mixed[window:], axis=0, keepdims=True)
    sine, cosine = sine_cosine(phase[...])
    energy[...] = energy[...] - PUSH_GAIN * (sampled[0] * cosine - sampled[1] * sine)
    phase[...] = phase[...] + PHASE_ADVANCE * energy[...]


def deposit(field, cell, hot, source):
    phase, row = cell[0], cell.at[3]
    rows = field.shape[1]
    half_rows = rows // 2
    groups = row.shape[0] // 2
    lanes = row.shape[1]
    sine, cosine = sine_cosine(phase)
    source[0] = SOURCE_GAIN * cosine
    source[1] = -SOURCE_GAIN * sine
    for half in range(2):
        row_ids = (lax.broadcasted_iota(jnp.int32, (half_rows, lanes), 0) + half * half_rows).astype(F32)
        total = None
        for group in range(groups):
            at = half * groups + group
            here = pl.ds(at, 1)
            match = row_ids == row[here, :]
            parts = []
            for part in range(2):
                high, low = split(jnp.where(match, source[part, here, :], 0.0))
                parts += [high, low]
            term = lax.dot_general(
                jnp.concatenate(parts, 0),
                hot[:, pl.ds(at * lanes, lanes)],
                (((1,), (1,)), ((), ())),
                preferred_element_type=F32,
            )
            total = term if total is None else total + term
        own = pl.ds(half * half_rows, half_rows)
        for part in range(2):
            first = total[2 * part * half_rows : (2 * part + 1) * half_rows]
            second = total[(2 * part + 1) * half_rows : (2 * part + 2) * half_rows]
            field[part, own, :] += first + second


def diffract(field, out, mat):
    rows, cols = field.shape[1], field.shape[2]
    mat_high, mat_low = mat[0], mat[1]
    wide_high = jnp.concatenate([mat_high[:cols], mat_high[cols:]], 1)
    wide_low = jnp.concatenate([mat_low[:cols], mat_low[cols:]], 1)
    high, low = split(field[...].reshape(2 * rows, cols))
    turned = dot(high, wide_high) + dot(high, wide_low) + dot(low, wide_high)
    real = turned[:rows, :cols] - turned[rows:, cols:]
    imag = turned[:rows, cols:] + turned[rows:, :cols]
    high, low = split(jnp.concatenate([real, imag], 1))
    turned = dot(mat_high, high) + dot(mat_high, low) + dot(mat_low, high)
    out[0] = turned[:rows, :cols] - turned[rows:, cols:]
    out[1] = turned[:rows, cols:] + turned[rows:, :cols]


def kernel(
    blocks, wave, phase_in, energy_in, offset_in, row_in, col_in, mat,
    wave_out, phase_out, energy_out,
    field, cells, pack, packed, leave, arrive, hot, sampled, source,
    near_sem, far_send, far_recv, part_send, part_recv, own_sem, hand_sem,
    out_send, out_recv, out_own, out_last, leave_send, leave_recv, leave_last,
):
    t, r = lax.axis_index("tm"), lax.axis_index("row")
    other = 1 - r
    after, before = lax.rem(t + 1, blocks), lax.rem(t + blocks - 1, blocks)
    slots = field.shape[0]
    half_rows = field.shape[2] // 2
    groups = cells.shape[2] // 2
    lanes = cells.shape[3]
    mine, theirs = pl.ds(r * half_rows, half_rows), pl.ds(other * half_rows, half_rows)
    inputs = (phase_in, energy_in, offset_in, row_in, col_in)

    def remote(src, dst, send, recv, where):
        return pltpu.make_async_remote_copy(
            src_ref=src, dst_ref=dst, send_sem=send, recv_sem=recv,
            device_id=where, device_id_type=pl.DeviceIdType.MESH,
        )

    def send_half(slot):
        item = slots * other + slot - 1
        return remote(wave.at[item], field.at[slot, :, mine, :], near_sem.at[0, slot], near_sem.at[1, slot], (t, other))

    def receive_half(slot):
        return remote(wave.at[0], field.at[slot, :, theirs, :], near_sem.at[0, slot], near_sem.at[1, slot], (t, other))

    def send_last(half):
        return remote(
            wave.at[wave.shape[0] - 1], field.at[0, :, pl.ds(half * half_rows, half_rows), :],
            far_send.at[0], far_recv.at[half], (after, 0),
        )

    def own_half(slot):
        return pltpu.make_async_copy(wave.at[slots * r + slot - 1], field.at[slot, :, mine, :], own_sem.at[slot])

    def send_part(slot):
        return remote(pack.at[slot], packed.at[slot], part_send.at[slot], part_recv.at[slot], (t, other))

    def hand_over():
        return remote(
            cells.at[0], cells.at[slots], hand_sem.at[0], hand_sem.at[1], (jnp.where(r == 1, t, before), other)
        )

    def is_last(slot):
        return (r == 1) & (slot == slots - 1)

    def goal(slot):
        last = is_last(slot)
        return jnp.where(last, after, t), jnp.where(last, 0, slots * r + slot + 1)

    def send_out(slot):
        block, item = goal(slot)
        return remote(
            field.at[slot, :, theirs, :], wave_out.at[item], out_send.at[slot], out_recv.at[item], (block, other)
        )

    def send_out_last():
        return remote(field.at[slots - 1, :, mine, :], wave_out.at[0], out_last.at[0], out_recv.at[0], (after, 1))

    def own_out(slot):
        return pltpu.make_async_copy(
            field.at[slot, :, mine, :], wave_out.at[slots * r + slot + 1], out_own.at[slot]
        )

    def send_leave(slot):
        block, item = goal(slot)
        return remote(
            leave.at[slot, other], arrive.at[item], leave_send.at[slot], leave_recv.at[item], (block, other)
        )

    def send_leave_last():
        return remote(leave.at[slots - 1, 1], arrive.at[0], leave_last.at[0], leave_recv.at[0], (after, 1))

    barrier = pltpu.get_barrier_semaphore()
    for peer in ((t, other), (after, 0), (after, 1), (before, 0), (before, 1)):
        pl.semaphore_signal(barrier, inc=1, device_id=peer, device_id_type=pl.DeviceIdType.MESH)

    @pl.loop(0, slots)
    def _(slot):
        for number, ref in enumerate(inputs):
            kept = ref[pl.ds(slots * r + slot, 1), :].astype(F32)
            sent = ref[pl.ds(slots * other + slot, 1), :].astype(F32)
            for group in range(groups):
                piece = slice(group * lanes, (group + 1) * lanes)
                cells[slot, number, pl.ds(r * groups + group, 1), :] = kept[:, piece]
                pack[slot, pl.ds(number * groups + group, 1), :] = sent[:, piece]

    pl.semaphore_wait(barrier, 5)

    @pl.when(t < blocks - 1)
    def _():
        send_last(r).start()

    for slot in range(slots):
        send_part(slot).start()
        if slot == 0:
            @pl.when(r == 0)
            def _():
                send_half(0).start()

            @pl.when(r == 1)
            def _():
                own_half(0).start()
        else:
            send_half(slot).start()
            own_half(slot).start()

    @pl.when((t == 0) & (r == 0))
    def _():
        field[0] = jnp.zeros(field.shape[1:], F32)

    @pl.loop(0, 2 * slots)
    def _(turn):
        ending = turn == 2 * slots - 1
        second = ((turn > 0) & (turn % 2 == 0)) | ending
        slot = jnp.where(ending, slots - 1, jnp.where(turn % 2 == 0, jnp.maximum(turn // 2 - 1, 0), (turn + 1) // 2))
        cell = slot + second.astype(jnp.int32)

        @pl.when(jnp.logical_not(second))
        def _():
            send_part(slot).wait_recv()
            for number in range(5):
                for group in range(groups):
                    cells[slot, number, pl.ds(other * groups + group, 1), :] = packed[
                        slot, pl.ds(number * groups + group, 1), :
                    ]

            @pl.when((r == 1) | (slot > 0))
            def _():
                own_half(slot).wait()
                receive_half(slot).wait_recv()

            @pl.when((r == 0) & (slot == 0) & (t > 0))
            def _():
                send_last(0).wait_recv()
                send_last(1).wait_recv()

        @pl.when(ending)
        def _():
            hand_over().wait_recv()

            @pl.when((r == 1) & (t == blocks - 1))
            def _():
                field[slots - 1] = jnp.zeros(field.shape[1:], F32)

        here = field.at[slot]
        push(here, cells.at[cell], hot, sampled)

        @pl.when(turn == 0)
        def _():
            hand_over().start()

        @pl.when(second)
        def _():
            for half in range(2):
                for number in range(2):
                    leave[slot, half, pl.ds(number * groups, groups), :] = cells[
                        cell, number, half * groups : (half + 1) * groups, :
                    ]
            send_leave(slot).start()

            @pl.when(is_last(slot))
            def _():
                send_leave_last().start()

            @pl.when(jnp.logical_not(is_last(slot)))
            def _():
                arrive[slots * r + slot + 1] = leave[slot, r]

        deposit(here, cells.at[cell], hot, source)
        diffract(here, here, mat)

        @pl.when(second)
        def _():
            send_out(slot).start()

            @pl.when(is_last(slot))
            def _():
                send_out_last().start()

            @pl.when(jnp.logical_not(is_last(slot)))
            def _():
                own_out(slot).start()

    def receive_leave(item):
        return remote(leave.at[0, 0], arrive.at[item], leave_send.at[0], leave_recv.at[item], (t, other))

    def receive_out(item):
        return remote(field.at[0, :, mine, :], wave_out.at[item], out_send.at[0], out_recv.at[item], (t, other))

    receive_leave(0).wait_recv()

    @pl.loop(0, slots)
    def _(slot):
        item = slots * other + slot + 1

        @pl.when(item < 2 * slots)
        def _():
            receive_leave(item).wait_recv()

    for item in range(2 * slots):
        for group in range(groups):
            piece = pl.ds(group * lanes, lanes)
            phase_out[pl.ds(item, 1), piece] = arrive[item, pl.ds(group, 1), :]
            energy_out[pl.ds(item, 1), piece] = arrive[item, pl.ds(groups + group, 1), :]

    @pl.when(t < blocks - 1)
    def _():
        send_last(r).wait_send()

    hand_over().wait_send()
    for slot in range(slots):
        send_part(slot).wait_send()
        if slot == 0:
            @pl.when(r == 0)
            def _():
                send_half(0).wait_send()
        else:
            send_half(slot).wait_send()
        send_leave(slot).wait_send()
        send_out(slot).wait_send()

        @pl.when(is_last(slot))
        def _():
            send_leave_last().wait_send()
            send_out_last().wait_send()

        @pl.when(jnp.logical_not(is_last(slot)))
        def _():
            own_out(slot).wait()

    receive_out(0).wait_recv()

    @pl.loop(0, slots)
    def _(slot):
        item = slots * other + slot + 1

        @pl.when(item < 2 * slots)
        def _():
            receive_out(item).wait_recv()


def body(wavefront, particle_phase, particle_energy, row_offset, row_cell, col_cell):
    items, _, half_rows, cols = wavefront.shape
    slots, rows = items // 2, 2 * half_rows
    width = particle_phase.shape[1]
    groups = width // LANES
    matrix = diffraction_matrix(cols)
    mat = jnp.asarray(np.stack(two_parts(np.concatenate([matrix.real, matrix.imag], 0))))
    vmem = pl.BlockSpec(memory_space=pltpu.VMEM)
    anywhere = pl.BlockSpec(memory_space=pl.ANY)
    dma = pltpu.SemaphoreType.DMA
    padded = -(-5 * groups // 8) * 8
    return pl.pallas_call(
        functools.partial(kernel, lax.axis_size("tm")),
        out_shape=(
            jax.ShapeDtypeStruct(wavefront.shape, F32),
            jax.ShapeDtypeStruct(particle_phase.shape, F32),
            jax.ShapeDtypeStruct(particle_phase.shape, F32),
        ),
        in_specs=[anywhere] + [vmem] * 6,
        out_specs=(anywhere, vmem, vmem),
        scratch_shapes=[
            pltpu.VMEM((slots, 2, rows, cols), F32),
            pltpu.VMEM((slots + 1, 5, 2 * groups, LANES), F32),
            pltpu.VMEM((slots, padded, LANES), F32),
            pltpu.VMEM((slots, padded, LANES), F32),
            pltpu.VMEM((slots, 2, 2 * groups, LANES), F32),
            pltpu.VMEM((items, 2 * groups, LANES), F32),
            pltpu.VMEM((cols, 2 * width), BF16),
            pltpu.VMEM((2, 2 * groups, LANES), F32),
            pltpu.VMEM((2, 2 * groups, LANES), F32),
            dma((2, slots)), dma((1,)), dma((2,)), dma((slots,)), dma((slots,)), dma((slots,)), dma((2,)),
            dma((slots,)), dma((items,)), dma((slots,)), dma((1,)), dma((slots,)), dma((items,)), dma((1,)),
        ],
        compiler_params=pltpu.CompilerParams(
            collective_id=0, has_side_effects=True, vmem_limit_bytes=48 * 1024 * 1024
        ),
        cost_estimate=pl.CostEstimate(flops=40 * 10**9, bytes_accessed=8 * 2**20, transcendentals=0),
    )(wavefront, particle_phase, particle_energy, row_offset, row_cell, col_cell, mat)


def solution(mesh):
    specs = (P("tm", None, "row", None),) + (P("tm", "row"),) * 5
    return jax.shard_map(body, mesh=mesh, in_specs=specs, out_specs=specs[:3], check_vma=False)
```

```python
import functools
import math

import jax
import jax.numpy as jnp
import ml_dtypes
import numpy as np
from jax import lax
from jax.experimental import pallas as pl
from jax.experimental.pallas import tpu as pltpu
from jax.sharding import PartitionSpec as P

PUSH_GAIN = 0.5
PHASE_ADVANCE = 1.0
SOURCE_GAIN = 1.0
LANES = 512
BF16 = jnp.bfloat16
F32 = jnp.float32


def diffraction_matrix(length):
    number = np.arange(length)
    signed = np.where(number < length // 2, number, number - length).astype(np.float64)
    kernel = np.fft.ifft(np.exp(-1j * math.pi / length * signed * signed))
    return kernel[(number[:, None] - number[None, :]) % length]


def two_parts(matrix):
    high = matrix.astype(ml_dtypes.bfloat16)
    low = (matrix - high.astype(np.float64)).astype(ml_dtypes.bfloat16)
    return high, low


def split(value):
    high = value.astype(BF16)
    return high, (value - high.astype(F32)).astype(BF16)


def sine_cosine(angle):
    count = jnp.round(angle * (2.0 / math.pi))
    rest = angle - count * 1.5703125
    rest = rest - count * 4.837512969970703125e-4
    rest = rest - count * 7.54978995489188216e-8
    quadrant = count.astype(jnp.int32)
    square = rest * rest
    sine = rest + rest * square * (
        -1.6666654611e-1 + square * (8.3321608736e-3 + square * -1.9515295891e-4)
    )
    cosine = 1.0 + square * (
        -0.5 + square * (4.166664568298827e-2 + square * (-1.388731625493765e-3 + square * 2.443315711809948e-5))
    )
    swapped = (quadrant & 1) == 1
    sine_out = jnp.where(swapped, cosine, sine)
    cosine_out = jnp.where(swapped, sine, cosine)
    sine_out = jnp.where((quadrant & 2) == 2, -sine_out, sine_out)
    cosine_out = jnp.where(((quadrant + 1) & 2) == 2, -cosine_out, cosine_out)
    return sine_out, cosine_out


def tiled(row, count):
    tile = jnp.broadcast_to(row, (16, row.shape[1])).astype(BF16)
    return jnp.concatenate([tile] * (count // 16), 0)


def dot(left, right):
    return jnp.dot(left, right, preferred_element_type=F32)


def push(field, cell, hot, sampled):
    phase, energy, offset, row, col = (cell.at[item] for item in range(5))
    rows, cols = field.shape[1], field.shape[2]
    half_rows = rows // 2
    window = half_rows + 16
    groups = row.shape[0] // 2
    lanes = row.shape[1]
    cells = lax.broadcasted_iota(jnp.int32, (cols, lanes), 0).astype(F32).astype(BF16)
    one, zero = jnp.ones((cols, lanes), BF16), jnp.zeros((cols, lanes), BF16)
    for half in range(2):
        start = 0 if half == 0 else half_rows - 16
        parts = jnp.concatenate(split(field[:, pl.ds(start, window), :].reshape(2 * window, cols)), 1)
        row_ids = (lax.broadcasted_iota(jnp.int32, (window, lanes), 0) + start).astype(F32)
        for group in range(groups):
            at = half * groups + group
            here = pl.ds(at, 1)
            one_hot = jnp.where(cells == tiled(col[here, :], cols), one, zero)
            hot[:, pl.ds(at * lanes, lanes)] = one_hot
            mixed = dot(parts, jnp.concatenate([one_hot, one_hot], 0))
            place = row[here, :]
            f = offset[here, :]
            weight = jnp.where(row_ids == place - 1.0, 0.5 * (0.5 - f) * (0.5 - f), 0.0)
            weight = jnp.where(row_ids == place, 0.75 - f * f, weight)
            weight = jnp.where(row_ids == place + 1.0, 0.5 * (0.5 + f) * (0.5 + f), weight)
            sampled[0, here, :] = jnp.sum(weight * mixed[:window], axis=0, keepdims=True)
            sampled[1, here, :] = jnp.sum(weight * mixed[window:], axis=0, keepdims=True)
    sine, cosine = sine_cosine(phase[...])
    energy[...] = energy[...] - PUSH_GAIN * (sampled[0] * cosine - sampled[1] * sine)
    phase[...] = phase[...] + PHASE_ADVANCE * energy[...]


def deposit(field, cell, hot, source):
    phase, row = cell[0], cell.at[3]
    rows = field.shape[1]
    half_rows = rows // 2
    groups = row.shape[0] // 2
    lanes = row.shape[1]
    sine, cosine = sine_cosine(phase)
    source[0] = SOURCE_GAIN * cosine
    source[1] = -SOURCE_GAIN * sine
    one, zero = jnp.ones((half_rows, lanes), BF16), jnp.zeros((half_rows, lanes), BF16)
    for half in range(2):
        row_ids = (lax.broadcasted_iota(jnp.int32, (half_rows, lanes), 0) + half * half_rows).astype(F32).astype(BF16)
        spread = []
        for group in range(groups):
            here = pl.ds(half * groups + group, 1)
            match = jnp.where(row_ids == tiled(row[here, :], half_rows), one, zero)
            parts = []
            for part in range(2):
                value = source[part, here, :]
                high = value.astype(BF16).astype(F32)
                parts += [match * tiled(high, half_rows), match * tiled(value - high, half_rows)]
            spread.append(jnp.concatenate(parts, 0))
        total = lax.dot_general(
            jnp.concatenate(spread, 1),
            hot[:, pl.ds(half * groups * lanes, groups * lanes)],
            (((1,), (1,)), ((), ())),
            preferred_element_type=F32,
        )
        own = pl.ds(half * half_rows, half_rows)
        for part in range(2):
            first = total[2 * part * half_rows : (2 * part + 1) * half_rows]
            second = total[(2 * part + 1) * half_rows : (2 * part + 2) * half_rows]
            field[part, own, :] += first + second


def diffract(field, out, mat):
    rows, cols = field.shape[1], field.shape[2]
    mat_high, mat_low = mat[0], mat[1]
    wide_high = jnp.concatenate([mat_high[:cols], mat_high[cols:]], 1)
    wide_low = jnp.concatenate([mat_low[:cols], mat_low[cols:]], 1)
    wide = jnp.concatenate([wide_high, wide_high, wide_low], 0)
    high, low = split(field[...].reshape(2 * rows, cols))
    turned = dot(jnp.concatenate([high, low, high], 1), wide)
    real = turned[:rows, :cols] - turned[rows:, cols:]
    imag = turned[:rows, cols:] + turned[rows:, :cols]
    high, low = split(jnp.concatenate([real, imag], 1))
    turned = dot(jnp.concatenate([mat_high, mat_high, mat_low], 1), jnp.concatenate([high, low, high], 0))
    out[0] = turned[:rows, :cols] - turned[rows:, cols:]
    out[1] = turned[:rows, cols:] + turned[rows:, :cols]


def kernel(
    blocks, wave, phase_hbm, energy_hbm, offset_hbm, row_hbm, col_hbm, mat_hbm,
    wave_out, phase_out, energy_out,
    field, cells, pack, packed, leave, arrive, hot, sampled, source,
    phase_in, energy_in, offset_in, row_in, col_in, mat, load_sem,
    near_sem, far_send, far_recv, part_send, part_recv, own_sem, hand_sem,
    out_send, out_recv, out_own, out_last, leave_send, leave_recv, leave_last,
):
    t, r = lax.axis_index("tm"), lax.axis_index("row")
    other = 1 - r
    after, before = lax.rem(t + 1, blocks), lax.rem(t + blocks - 1, blocks)
    slots = field.shape[0]
    half_rows = field.shape[2] // 2
    groups = cells.shape[2] // 2
    lanes = cells.shape[3]
    mine, theirs = pl.ds(r * half_rows, half_rows), pl.ds(other * half_rows, half_rows)
    inputs = (phase_in, energy_in, offset_in, row_in, col_in)
    sources = (phase_hbm, energy_hbm, offset_hbm, row_hbm, col_hbm, mat_hbm)
    loads = [
        pltpu.make_async_copy(src, dst, load_sem.at[number])
        for number, (src, dst) in enumerate(zip(sources, inputs + (mat,)))
    ]
    for load in loads:
        load.start()

    def remote(src, dst, send, recv, where):
        return pltpu.make_async_remote_copy(
            src_ref=src, dst_ref=dst, send_sem=send, recv_sem=recv,
            device_id=where, device_id_type=pl.DeviceIdType.MESH,
        )

    def send_half(slot):
        item = slots * other + slot - 1
        return remote(wave.at[item], field.at[slot, :, mine, :], near_sem.at[0, slot], near_sem.at[1, slot], (t, other))

    def receive_half(slot):
        return remote(wave.at[0], field.at[slot, :, theirs, :], near_sem.at[0, slot], near_sem.at[1, slot], (t, other))

    def send_last(half):
        return remote(
            wave.at[wave.shape[0] - 1], field.at[0, :, pl.ds(half * half_rows, half_rows), :],
            far_send.at[0], far_recv.at[half], (after, 0),
        )

    def own_half(slot):
        return pltpu.make_async_copy(wave.at[slots * r + slot - 1], field.at[slot, :, mine, :], own_sem.at[slot])

    def send_part(slot):
        return remote(pack.at[slot], packed.at[slot], part_send.at[slot], part_recv.at[slot], (t, other))

    def hand_over():
        return remote(
            cells.at[0], cells.at[slots], hand_sem.at[0], hand_sem.at[1], (jnp.where(r == 1, t, before), other)
        )

    def is_last(slot):
        return (r == 1) & (slot == slots - 1)

    def goal(slot):
        last = is_last(slot)
        return jnp.where(last, after, t), jnp.where(last, 0, slots * r + slot + 1)

    def send_out(slot):
        block, item = goal(slot)
        return remote(
            field.at[slot, :, theirs, :], wave_out.at[item], out_send.at[slot], out_recv.at[item], (block, other)
        )

    def send_out_last():
        return remote(field.at[slots - 1, :, mine, :], wave_out.at[0], out_last.at[0], out_recv.at[0], (after, 1))

    def own_out(slot):
        return pltpu.make_async_copy(
            field.at[slot, :, mine, :], wave_out.at[slots * r + slot + 1], out_own.at[slot]
        )

    def send_leave(slot):
        block, item = goal(slot)
        return remote(
            leave.at[slot, other], arrive.at[item], leave_send.at[slot], leave_recv.at[item], (block, other)
        )

    def send_leave_last():
        return remote(leave.at[slots - 1, 1], arrive.at[0], leave_last.at[0], leave_recv.at[0], (after, 1))

    barrier = pltpu.get_barrier_semaphore()
    for peer in ((t, other), (after, 0), (after, 1), (before, 0), (before, 1)):
        pl.semaphore_signal(barrier, inc=1, device_id=peer, device_id_type=pl.DeviceIdType.MESH)

    for load in loads[:-1]:
        load.wait()

    @pl.loop(0, slots)
    def _(slot):
        for number, ref in enumerate(inputs):
            kept = ref[pl.ds(slots * r + slot, 1), :].astype(F32)
            sent = ref[pl.ds(slots * other + slot, 1), :].astype(F32)
            for group in range(groups):
                piece = slice(group * lanes, (group + 1) * lanes)
                cells[slot, number, pl.ds(r * groups + group, 1), :] = kept[:, piece]
                pack[slot, pl.ds(number * groups + group, 1), :] = sent[:, piece]

    pl.semaphore_wait(barrier, 5)

    @pl.when(t < blocks - 1)
    def _():
        send_last(r).start()

    for slot in range(slots):
        send_part(slot).start()
        if slot == 0:
            @pl.when(r == 0)
            def _():
                send_half(0).start()

            @pl.when(r == 1)
            def _():
                own_half(0).start()
        else:
            send_half(slot).start()
            own_half(slot).start()

    @pl.when((t == 0) & (r == 0))
    def _():
        field[0] = jnp.zeros(field.shape[1:], F32)

    @pl.loop(0, 2 * slots)
    def _(turn):
        ending = turn == 2 * slots - 1
        second = ((turn > 0) & (turn % 2 == 0)) | ending
        slot = jnp.where(ending, slots - 1, jnp.where(turn % 2 == 0, jnp.maximum(turn // 2 - 1, 0), (turn + 1) // 2))
        cell = slot + second.astype(jnp.int32)

        @pl.when(jnp.logical_not(second))
        def _():
            send_part(slot).wait_recv()
            for number in range(5):
                for group in range(groups):
                    cells[slot, number, pl.ds(other * groups + group, 1), :] = packed[
                        slot, pl.ds(number * groups + group, 1), :
                    ]

            @pl.when((r == 1) | (slot > 0))
            def _():
                own_half(slot).wait()
                receive_half(slot).wait_recv()

            @pl.when((r == 0) & (slot == 0) & (t > 0))
            def _():
                send_last(0).wait_recv()
                send_last(1).wait_recv()

        @pl.when(ending)
        def _():
            hand_over().wait_recv()

            @pl.when((r == 1) & (t == blocks - 1))
            def _():
                field[slots - 1] = jnp.zeros(field.shape[1:], F32)

        here = field.at[slot]
        push(here, cells.at[cell], hot, sampled)

        @pl.when(turn == 0)
        def _():
            hand_over().start()

        @pl.when(second)
        def _():
            for half in range(2):
                for number in range(2):
                    leave[slot, half, pl.ds(number * groups, groups), :] = cells[
                        cell, number, half * groups : (half + 1) * groups, :
                    ]
            send_leave(slot).start()

            @pl.when(is_last(slot))
            def _():
                send_leave_last().start()

            @pl.when(jnp.logical_not(is_last(slot)))
            def _():
                arrive[slots * r + slot + 1] = leave[slot, r]

        deposit(here, cells.at[cell], hot, source)

        @pl.when(turn == 0)
        def _():
            loads[-1].wait()

        diffract(here, here, mat)

        @pl.when(second)
        def _():
            send_out(slot).start()

            @pl.when(is_last(slot))
            def _():
                send_out_last().start()

            @pl.when(jnp.logical_not(is_last(slot)))
            def _():
                own_out(slot).start()

    def receive_leave(item):
        return remote(leave.at[0, 0], arrive.at[item], leave_send.at[0], leave_recv.at[item], (t, other))

    def receive_out(item):
        return remote(field.at[0, :, mine, :], wave_out.at[item], out_send.at[0], out_recv.at[item], (t, other))

    receive_leave(0).wait_recv()

    @pl.loop(0, slots)
    def _(slot):
        item = slots * other + slot + 1

        @pl.when(item < 2 * slots)
        def _():
            receive_leave(item).wait_recv()

    for item in range(2 * slots):
        for group in range(groups):
            piece = pl.ds(group * lanes, lanes)
            phase_out[pl.ds(item, 1), piece] = arrive[item, pl.ds(group, 1), :]
            energy_out[pl.ds(item, 1), piece] = arrive[item, pl.ds(groups + group, 1), :]

    @pl.when(t < blocks - 1)
    def _():
        send_last(r).wait_send()

    hand_over().wait_send()
    for slot in range(slots):
        send_part(slot).wait_send()
        if slot == 0:
            @pl.when(r == 0)
            def _():
                send_half(0).wait_send()
        else:
            send_half(slot).wait_send()
        send_leave(slot).wait_send()
        send_out(slot).wait_send()

        @pl.when(is_last(slot))
        def _():
            send_leave_last().wait_send()
            send_out_last().wait_send()

        @pl.when(jnp.logical_not(is_last(slot)))
        def _():
            own_out(slot).wait()

    receive_out(0).wait_recv()

    @pl.loop(0, slots)
    def _(slot):
        item = slots * other + slot + 1

        @pl.when(item < 2 * slots)
        def _():
            receive_out(item).wait_recv()


def body(wavefront, particle_phase, particle_energy, row_offset, row_cell, col_cell):
    items, _, half_rows, cols = wavefront.shape
    slots, rows = items // 2, 2 * half_rows
    width = particle_phase.shape[1]
    groups = width // LANES
    matrix = diffraction_matrix(cols)
    mat = jnp.asarray(np.stack(two_parts(np.concatenate([matrix.real, matrix.imag], 0))))
    vmem = pl.BlockSpec(memory_space=pltpu.VMEM)
    anywhere = pl.BlockSpec(memory_space=pl.ANY)
    dma = pltpu.SemaphoreType.DMA
    padded = -(-5 * groups // 8) * 8
    return pl.pallas_call(
        functools.partial(kernel, lax.axis_size("tm")),
        out_shape=(
            jax.ShapeDtypeStruct(wavefront.shape, F32),
            jax.ShapeDtypeStruct(particle_phase.shape, F32),
            jax.ShapeDtypeStruct(particle_phase.shape, F32),
        ),
        in_specs=[anywhere] * 7,
        out_specs=(anywhere, vmem, vmem),
        scratch_shapes=[
            pltpu.VMEM((slots, 2, rows, cols), F32),
            pltpu.VMEM((slots + 1, 5, 2 * groups, LANES), F32),
            pltpu.VMEM((slots, padded, LANES), F32),
            pltpu.VMEM((slots, padded, LANES), F32),
            pltpu.VMEM((slots, 2, 2 * groups, LANES), F32),
            pltpu.VMEM((items, 2 * groups, LANES), F32),
            pltpu.VMEM((cols, 2 * width), BF16),
            pltpu.VMEM((2, 2 * groups, LANES), F32),
            pltpu.VMEM((2, 2 * groups, LANES), F32),
            *[pltpu.VMEM(particle_phase.shape, F32)] * 3,
            *[pltpu.VMEM(particle_phase.shape, jnp.int32)] * 2,
            pltpu.VMEM(mat.shape, BF16),
            dma((6,)),
            dma((2, slots)), dma((1,)), dma((2,)), dma((slots,)), dma((slots,)), dma((slots,)), dma((2,)),
            dma((slots,)), dma((items,)), dma((slots,)), dma((1,)), dma((slots,)), dma((items,)), dma((1,)),
        ],
        compiler_params=pltpu.CompilerParams(
            collective_id=0, has_side_effects=True, vmem_limit_bytes=60 * 1024 * 1024
        ),
        cost_estimate=pl.CostEstimate(flops=40 * 10**9, bytes_accessed=8 * 2**20, transcendentals=0),
    )(wavefront, particle_phase, particle_energy, row_offset, row_cell, col_cell, mat)


def solution(mesh):
    specs = (P("tm", None, "row", None),) + (P("tm", "row"),) * 5
    return jax.shard_map(body, mesh=mesh, in_specs=specs, out_specs=specs[:3], check_vma=False)
```

```python
import functools
import math

import jax
import jax.numpy as jnp
import ml_dtypes
import numpy as np
from jax import lax
from jax.experimental import pallas as pl
from jax.experimental.pallas import tpu as pltpu
from jax.sharding import PartitionSpec as P

PUSH_GAIN = 0.5
PHASE_ADVANCE = 1.0
SOURCE_GAIN = 1.0
LANES = 512
BF16 = jnp.bfloat16
F32 = jnp.float32


def diffraction_matrix(length):
    number = np.arange(length)
    signed = np.where(number < length // 2, number, number - length).astype(np.float64)
    kernel = np.fft.ifft(np.exp(-1j * math.pi / length * signed * signed))
    return kernel[(number[:, None] - number[None, :]) % length]


def two_parts(matrix):
    high = matrix.astype(ml_dtypes.bfloat16)
    low = (matrix - high.astype(np.float64)).astype(ml_dtypes.bfloat16)
    return high, low


def split(value):
    high = value.astype(BF16)
    return high, (value - high.astype(F32)).astype(BF16)


def sine_cosine(angle):
    count = jnp.round(angle * (2.0 / math.pi))
    rest = angle - count * 1.5703125
    rest = rest - count * 4.837512969970703125e-4
    rest = rest - count * 7.54978995489188216e-8
    quadrant = count.astype(jnp.int32)
    square = rest * rest
    sine = rest + rest * square * (
        -1.6666654611e-1 + square * (8.3321608736e-3 + square * -1.9515295891e-4)
    )
    cosine = 1.0 + square * (
        -0.5 + square * (4.166664568298827e-2 + square * (-1.388731625493765e-3 + square * 2.443315711809948e-5))
    )
    swapped = (quadrant & 1) == 1
    sine_out = jnp.where(swapped, cosine, sine)
    cosine_out = jnp.where(swapped, sine, cosine)
    sine_out = jnp.where((quadrant & 2) == 2, -sine_out, sine_out)
    cosine_out = jnp.where(((quadrant + 1) & 2) == 2, -cosine_out, cosine_out)
    return sine_out, cosine_out


def tiled(row, count):
    tile = jnp.broadcast_to(row, (16, row.shape[1])).astype(BF16)
    return jnp.concatenate([tile] * (count // 16), 0)


def dot(left, right):
    return jnp.dot(left, right, preferred_element_type=F32)


def push(field, cell, hot, sampled):
    phase, energy, offset, row, col = (cell.at[item] for item in range(5))
    rows, cols = field.shape[1], field.shape[2]
    half_rows = rows // 2
    window = half_rows + 16
    groups = row.shape[0] // 2
    lanes = row.shape[1]
    cells = lax.broadcasted_iota(jnp.int32, (cols, lanes), 0).astype(F32).astype(BF16)
    one, zero = jnp.ones((cols, lanes), BF16), jnp.zeros((cols, lanes), BF16)
    for half in range(2):
        start = 0 if half == 0 else half_rows - 16
        parts = jnp.concatenate(split(field[:, pl.ds(start, window), :].reshape(2 * window, cols)), 1)
        row_ids = (lax.broadcasted_iota(jnp.int32, (window, lanes), 0) + start).astype(F32)
        for group in range(groups):
            at = half * groups + group
            here = pl.ds(at, 1)
            one_hot = jnp.where(cells == tiled(col[here, :], cols), one, zero)
            hot[:, pl.ds(at * lanes, lanes)] = one_hot
            mixed = dot(parts, jnp.concatenate([one_hot, one_hot], 0))
            place = row[here, :]
            f = offset[here, :]
            weight = jnp.where(row_ids == place - 1.0, 0.5 * (0.5 - f) * (0.5 - f), 0.0)
            weight = jnp.where(row_ids == place, 0.75 - f * f, weight)
            weight = jnp.where(row_ids == place + 1.0, 0.5 * (0.5 + f) * (0.5 + f), weight)
            sampled[0, here, :] = jnp.sum(weight * mixed[:window], axis=0, keepdims=True)
            sampled[1, here, :] = jnp.sum(weight * mixed[window:], axis=0, keepdims=True)
    sine, cosine = sine_cosine(phase[...])
    energy[...] = energy[...] - PUSH_GAIN * (sampled[0] * cosine - sampled[1] * sine)
    phase[...] = phase[...] + PHASE_ADVANCE * energy[...]


def deposit(field, cell, hot, source):
    phase, row = cell[0], cell.at[3]
    rows = field.shape[1]
    half_rows = rows // 2
    groups = row.shape[0] // 2
    lanes = row.shape[1]
    sine, cosine = sine_cosine(phase)
    source[0] = SOURCE_GAIN * cosine
    source[1] = -SOURCE_GAIN * sine
    one, zero = jnp.ones((half_rows, lanes), BF16), jnp.zeros((half_rows, lanes), BF16)
    for half in range(2):
        row_ids = (lax.broadcasted_iota(jnp.int32, (half_rows, lanes), 0) + half * half_rows).astype(F32).astype(BF16)
        spread = []
        for group in range(groups):
            here = pl.ds(half * groups + group, 1)
            match = jnp.where(row_ids == tiled(row[here, :], half_rows), one, zero)
            parts = []
            for part in range(2):
                value = source[part, here, :]
                high = value.astype(BF16).astype(F32)
                parts += [match * tiled(high, half_rows), match * tiled(value - high, half_rows)]
            spread.append(jnp.concatenate(parts, 0))
        total = lax.dot_general(
            jnp.concatenate(spread, 1),
            hot[:, pl.ds(half * groups * lanes, groups * lanes)],
            (((1,), (1,)), ((), ())),
            preferred_element_type=F32,
        )
        own = pl.ds(half * half_rows, half_rows)
        for part in range(2):
            first = total[2 * part * half_rows : (2 * part + 1) * half_rows]
            second = total[(2 * part + 1) * half_rows : (2 * part + 2) * half_rows]
            field[part, own, :] += first + second


def diffract(field, out, mat):
    rows, cols = field.shape[1], field.shape[2]
    mat_high, mat_low = mat[0], mat[1]
    wide_high = jnp.concatenate([mat_high[:cols], mat_high[cols:]], 1)
    wide_low = jnp.concatenate([mat_low[:cols], mat_low[cols:]], 1)
    wide = jnp.concatenate([wide_high, wide_high, wide_low], 0)
    high, low = split(field[...].reshape(2 * rows, cols))
    turned = dot(jnp.concatenate([high, low, high], 1), wide)
    real = turned[:rows, :cols] - turned[rows:, cols:]
    imag = turned[:rows, cols:] + turned[rows:, :cols]
    high, low = split(jnp.concatenate([real, imag], 1))
    turned = dot(jnp.concatenate([mat_high, mat_high, mat_low], 1), jnp.concatenate([high, low, high], 0))
    out[0] = turned[:rows, :cols] - turned[rows:, cols:]
    out[1] = turned[:rows, cols:] + turned[rows:, :cols]


def kernel(
    blocks, wave, phase_hbm, energy_hbm, offset_hbm, row_hbm, col_hbm, mat_hbm,
    wave_out, phase_out, energy_out,
    field, cells, pack, packed, leave, arrive, hot, sampled, source,
    phase_in, energy_in, offset_in, row_in, col_in, mat, load_sem,
    near_sem, far_send, far_recv, part_send, part_recv, own_sem, hand_sem,
    out_send, out_recv, out_own, out_last, leave_send, leave_recv, leave_last,
):
    t, r = lax.axis_index("tm"), lax.axis_index("row")
    other = 1 - r
    after, before = lax.rem(t + 1, blocks), lax.rem(t + blocks - 1, blocks)
    slots = field.shape[0]
    half_rows = field.shape[2] // 2
    groups = cells.shape[2] // 2
    lanes = cells.shape[3]
    mine, theirs = pl.ds(r * half_rows, half_rows), pl.ds(other * half_rows, half_rows)
    inputs = (phase_in, energy_in, offset_in, row_in, col_in)
    sources = (phase_hbm, energy_hbm, offset_hbm, row_hbm, col_hbm, mat_hbm)
    loads = [
        pltpu.make_async_copy(src, dst, load_sem.at[number])
        for number, (src, dst) in enumerate(zip(sources, inputs + (mat,)))
    ]
    for load in loads:
        load.start()

    def remote(src, dst, send, recv, where):
        return pltpu.make_async_remote_copy(
            src_ref=src, dst_ref=dst, send_sem=send, recv_sem=recv,
            device_id=where, device_id_type=pl.DeviceIdType.MESH,
        )

    def send_half(slot):
        item = slots * other + slot - 1
        return remote(wave.at[item], field.at[slot, :, mine, :], near_sem.at[0, slot], near_sem.at[1, slot], (t, other))

    def receive_half(slot):
        return remote(wave.at[0], field.at[slot, :, theirs, :], near_sem.at[0, slot], near_sem.at[1, slot], (t, other))

    def send_last(half):
        return remote(
            wave.at[wave.shape[0] - 1], field.at[0, :, pl.ds(half * half_rows, half_rows), :],
            far_send.at[0], far_recv.at[half], (after, 0),
        )

    def own_half(slot):
        return pltpu.make_async_copy(wave.at[slots * r + slot - 1], field.at[slot, :, mine, :], own_sem.at[slot])

    def send_part(pair):
        return remote(pack.at[pair], packed.at[pair], part_send.at[pair], part_recv.at[pair], (t, other))

    def pack_pair(pair):
        for slot in range(2 * pair, 2 * pair + 2):
            for number, ref in enumerate(inputs):
                kept = ref[pl.ds(slots * r + slot, 1), :].astype(F32)
                sent = ref[pl.ds(slots * other + slot, 1), :].astype(F32)
                base = ((slot % 2) * 5 + number) * groups
                for group in range(groups):
                    piece = slice(group * lanes, (group + 1) * lanes)
                    cells[slot, number, pl.ds(r * groups + group, 1), :] = kept[:, piece]
                    pack[pair, pl.ds(base + group, 1), :] = sent[:, piece]

    def hand_over():
        return remote(
            cells.at[0], cells.at[slots], hand_sem.at[0], hand_sem.at[1], (jnp.where(r == 1, t, before), other)
        )

    def is_last(slot):
        return (r == 1) & (slot == slots - 1)

    def goal(slot):
        last = is_last(slot)
        return jnp.where(last, after, t), jnp.where(last, 0, slots * r + slot + 1)

    def send_out(slot):
        block, item = goal(slot)
        return remote(
            field.at[slot, :, theirs, :], wave_out.at[item], out_send.at[slot], out_recv.at[item], (block, other)
        )

    def send_out_last():
        return remote(field.at[slots - 1, :, mine, :], wave_out.at[0], out_last.at[0], out_recv.at[0], (after, 1))

    def own_out(slot):
        return pltpu.make_async_copy(
            field.at[slot, :, mine, :], wave_out.at[slots * r + slot + 1], out_own.at[slot]
        )

    def send_leave(slot):
        block, item = goal(slot)
        return remote(
            leave.at[slot, other], arrive.at[item], leave_send.at[slot], leave_recv.at[item], (block, other)
        )

    def send_leave_last():
        return remote(leave.at[slots - 1, 1], arrive.at[0], leave_last.at[0], leave_recv.at[0], (after, 1))

    barrier = pltpu.get_barrier_semaphore()
    for peer in ((t, other), (after, 0), (after, 1), (before, 0), (before, 1)):
        pl.semaphore_signal(barrier, inc=1, device_id=peer, device_id_type=pl.DeviceIdType.MESH)

    pl.semaphore_wait(barrier, 5)

    @pl.when(t < blocks - 1)
    def _():
        send_last(r).start()

    @pl.when(r == 0)
    def _():
        send_half(0).start()

    @pl.when(r == 1)
    def _():
        own_half(0).start()

    for load in loads[:-1]:
        load.wait()
    pack_pair(0)
    send_part(0).start()
    send_half(1).start()
    for pair in range(1, slots // 2):
        pack_pair(pair)
    for slot in range(1, slots):
        own_half(slot).start()

    @pl.when((t == 0) & (r == 0))
    def _():
        field[0] = jnp.zeros(field.shape[1:], F32)

    @pl.loop(0, 2 * slots)
    def _(turn):
        ending = turn == 2 * slots - 1
        second = ((turn > 0) & (turn % 2 == 0)) | ending
        slot = jnp.where(ending, slots - 1, jnp.where(turn % 2 == 0, jnp.maximum(turn // 2 - 1, 0), (turn + 1) // 2))
        cell = slot + second.astype(jnp.int32)

        @pl.when(jnp.logical_not(second))
        def _():
            pair, base = slot // 2, (slot % 2) * (5 * groups)

            @pl.when(slot % 2 == 0)
            def _():
                send_part(pair).wait_recv()

            for number in range(5):
                for group in range(groups):
                    cells[slot, number, pl.ds(other * groups + group, 1), :] = packed[
                        pair, pl.ds(base + number * groups + group, 1), :
                    ]

            @pl.when((r == 1) | (slot > 0))
            def _():
                own_half(slot).wait()
                receive_half(slot).wait_recv()

            @pl.when((r == 0) & (slot == 0) & (t > 0))
            def _():
                send_last(0).wait_recv()
                send_last(1).wait_recv()

            @pl.when((slot > 0) | (r == 0))
            def _():
                send_half(slot).wait_send()

            @pl.when((slot == 0) & (r == 1) & (t < blocks - 1))
            def _():
                send_last(r).wait_send()

            @pl.when(slot < slots - 2)
            def _():
                @pl.when(slot % 2 == 0)
                def _():
                    send_part(pair + 1).start()

                send_half(slot + 2).start()

        @pl.when(ending)
        def _():
            hand_over().wait_recv()

            @pl.when((r == 1) & (t == blocks - 1))
            def _():
                field[slots - 1] = jnp.zeros(field.shape[1:], F32)

        here = field.at[slot]
        push(here, cells.at[cell], hot, sampled)

        @pl.when(turn == 0)
        def _():
            hand_over().start()

        @pl.when(second)
        def _():
            for half in range(2):
                for number in range(2):
                    leave[slot, half, pl.ds(number * groups, groups), :] = cells[
                        cell, number, half * groups : (half + 1) * groups, :
                    ]
            send_leave(slot).start()

            @pl.when(is_last(slot))
            def _():
                send_leave_last().start()

            @pl.when(jnp.logical_not(is_last(slot)))
            def _():
                arrive[slots * r + slot + 1] = leave[slot, r]

        deposit(here, cells.at[cell], hot, source)

        @pl.when(turn == 0)
        def _():
            loads[-1].wait()

        diffract(here, here, mat)

        @pl.when(second)
        def _():
            send_out(slot).start()

            @pl.when(is_last(slot))
            def _():
                send_out_last().start()

            @pl.when(jnp.logical_not(is_last(slot)))
            def _():
                own_out(slot).start()

    def receive_leave(item):
        return remote(leave.at[0, 0], arrive.at[item], leave_send.at[0], leave_recv.at[item], (t, other))

    def receive_out(item):
        return remote(field.at[0, :, mine, :], wave_out.at[item], out_send.at[0], out_recv.at[item], (t, other))

    receive_leave(0).wait_recv()

    @pl.loop(0, slots)
    def _(slot):
        item = slots * other + slot + 1

        @pl.when(item < 2 * slots)
        def _():
            receive_leave(item).wait_recv()

    for item in range(2 * slots):
        for group in range(groups):
            piece = pl.ds(group * lanes, lanes)
            phase_out[pl.ds(item, 1), piece] = arrive[item, pl.ds(group, 1), :]
            energy_out[pl.ds(item, 1), piece] = arrive[item, pl.ds(groups + group, 1), :]

    @pl.when((r == 0) & (t < blocks - 1))
    def _():
        send_last(r).wait_send()

    hand_over().wait_send()
    for pair in range(slots // 2):
        send_part(pair).wait_send()
    for slot in range(slots):
        send_leave(slot).wait_send()
        send_out(slot).wait_send()

        @pl.when(is_last(slot))
        def _():
            send_leave_last().wait_send()
            send_out_last().wait_send()

        @pl.when(jnp.logical_not(is_last(slot)))
        def _():
            own_out(slot).wait()

    receive_out(0).wait_recv()

    @pl.loop(0, slots)
    def _(slot):
        item = slots * other + slot + 1

        @pl.when(item < 2 * slots)
        def _():
            receive_out(item).wait_recv()


def body(wavefront, particle_phase, particle_energy, row_offset, row_cell, col_cell):
    items, _, half_rows, cols = wavefront.shape
    slots, rows = items // 2, 2 * half_rows
    width = particle_phase.shape[1]
    groups = width // LANES
    matrix = diffraction_matrix(cols)
    mat = jnp.asarray(np.stack(two_parts(np.concatenate([matrix.real, matrix.imag], 0))))
    vmem = pl.BlockSpec(memory_space=pltpu.VMEM)
    anywhere = pl.BlockSpec(memory_space=pl.ANY)
    dma = pltpu.SemaphoreType.DMA
    return pl.pallas_call(
        functools.partial(kernel, lax.axis_size("tm")),
        out_shape=(
            jax.ShapeDtypeStruct(wavefront.shape, F32),
            jax.ShapeDtypeStruct(particle_phase.shape, F32),
            jax.ShapeDtypeStruct(particle_phase.shape, F32),
        ),
        in_specs=[pl.BlockSpec(memory_space=pltpu.HBM)] * 7,
        out_specs=(anywhere, vmem, vmem),
        scratch_shapes=[
            pltpu.VMEM((slots, 2, rows, cols), F32),
            pltpu.VMEM((slots + 1, 5, 2 * groups, LANES), F32),
            pltpu.VMEM((slots // 2, 10 * groups, LANES), F32),
            pltpu.VMEM((slots // 2, 10 * groups, LANES), F32),
            pltpu.VMEM((slots, 2, 2 * groups, LANES), F32),
            pltpu.VMEM((items, 2 * groups, LANES), F32),
            pltpu.VMEM((cols, 2 * width), BF16),
            pltpu.VMEM((2, 2 * groups, LANES), F32),
            pltpu.VMEM((2, 2 * groups, LANES), F32),
            *[pltpu.VMEM(particle_phase.shape, F32)] * 3,
            *[pltpu.VMEM(particle_phase.shape, jnp.int32)] * 2,
            pltpu.VMEM(mat.shape, BF16),
            dma((6,)),
            dma((2, slots)), dma((1,)), dma((2,)), dma((slots // 2,)), dma((slots // 2,)), dma((slots,)), dma((2,)),
            dma((slots,)), dma((items,)), dma((slots,)), dma((1,)), dma((slots,)), dma((items,)), dma((1,)),
        ],
        compiler_params=pltpu.CompilerParams(
            collective_id=0, has_side_effects=True, vmem_limit_bytes=48 * 1024 * 1024
        ),
        cost_estimate=pl.CostEstimate(flops=40 * 10**9, bytes_accessed=8 * 2**20, transcendentals=0),
    )(wavefront, particle_phase, particle_energy, row_offset, row_cell, col_cell, mat)


def solution(mesh):
    specs = (P("tm", None, "row", None),) + (P("tm", "row"),) * 5
    return jax.shard_map(body, mesh=mesh, in_specs=specs, out_specs=specs[:3], check_vma=False)
```

```python
import functools
import math

import jax
import jax.numpy as jnp
from jax import lax
from jax.experimental import pallas as pl
from jax.experimental.pallas import tpu as pltpu
from jax.sharding import PartitionSpec as P

PUSH_GAIN = 0.5
PHASE_ADVANCE = 1.0
SOURCE_GAIN = 1.0
LANES = 512
BF16 = jnp.bfloat16
F32 = jnp.float32


def split(value):
    high = value.astype(BF16)
    return high, (value - high.astype(F32)).astype(BF16)


def sine_cosine(angle):
    count = jnp.round(angle * (2.0 / math.pi))
    rest = angle - count * 1.5703125
    rest = rest - count * 4.837512969970703125e-4
    rest = rest - count * 7.54978995489188216e-8
    quadrant = count.astype(jnp.int32)
    square = rest * rest
    sine = rest + rest * square * (
        -1.6666654611e-1 + square * (8.3321608736e-3 + square * -1.9515295891e-4)
    )
    cosine = 1.0 + square * (
        -0.5 + square * (4.166664568298827e-2 + square * (-1.388731625493765e-3 + square * 2.443315711809948e-5))
    )
    swapped = (quadrant & 1) == 1
    sine_out = jnp.where(swapped, cosine, sine)
    cosine_out = jnp.where(swapped, sine, cosine)
    sine_out = jnp.where((quadrant & 2) == 2, -sine_out, sine_out)
    cosine_out = jnp.where(((quadrant + 1) & 2) == 2, -cosine_out, cosine_out)
    return sine_out, cosine_out


def tiled(row, count):
    tile = jnp.broadcast_to(row, (16, row.shape[1])).astype(BF16)
    return jnp.concatenate([tile] * (count // 16), 0)


def fill_matrix(mat):
    length = mat.shape[2]
    away = lax.broadcasted_iota(jnp.int32, (length, length), 0) - lax.broadcasted_iota(jnp.int32, (length, length), 1)
    turn = lax.rem(away * away, 2 * length).astype(F32)
    sine, cosine = sine_cosine((math.pi / length) * turn - math.pi / 4)
    for number, value in enumerate((cosine, sine)):
        for part, piece in enumerate(split(value * (1.0 / math.sqrt(length)))):
            mat[part, pl.ds(number * length, length), :] = piece


def dot(left, right):
    return jnp.dot(left, right, preferred_element_type=F32)


def push(field, cell, hot, sampled):
    phase, energy, offset, row, col = (cell.at[item] for item in range(5))
    rows, cols = field.shape[1], field.shape[2]
    half_rows = rows // 2
    window = half_rows + 16
    groups = row.shape[0] // 2
    lanes = row.shape[1]
    cells = lax.broadcasted_iota(jnp.int32, (cols, lanes), 0).astype(F32).astype(BF16)
    one, zero = jnp.ones((cols, lanes), BF16), jnp.zeros((cols, lanes), BF16)
    for half in range(2):
        start = 0 if half == 0 else half_rows - 16
        parts = jnp.concatenate(split(field[:, pl.ds(start, window), :].reshape(2 * window, cols)), 1)
        row_ids = (lax.broadcasted_iota(jnp.int32, (window, lanes), 0) + start).astype(F32)
        for group in range(groups):
            at = half * groups + group
            here = pl.ds(at, 1)
            one_hot = jnp.where(cells == tiled(col[here, :], cols), one, zero)
            hot[:, pl.ds(at * lanes, lanes)] = one_hot
            mixed = dot(parts, jnp.concatenate([one_hot, one_hot], 0))
            place = row[here, :]
            f = offset[here, :]
            weight = jnp.where(row_ids == place - 1.0, 0.5 * (0.5 - f) * (0.5 - f), 0.0)
            weight = jnp.where(row_ids == place, 0.75 - f * f, weight)
            weight = jnp.where(row_ids == place + 1.0, 0.5 * (0.5 + f) * (0.5 + f), weight)
            sampled[0, here, :] = jnp.sum(weight * mixed[:window], axis=0, keepdims=True)
            sampled[1, here, :] = jnp.sum(weight * mixed[window:], axis=0, keepdims=True)
    sine, cosine = sine_cosine(phase[...])
    energy[...] = energy[...] - PUSH_GAIN * (sampled[0] * cosine - sampled[1] * sine)
    phase[...] = phase[...] + PHASE_ADVANCE * energy[...]


def deposit(field, cell, hot, source):
    phase, row = cell[0], cell.at[3]
    rows = field.shape[1]
    half_rows = rows // 2
    groups = row.shape[0] // 2
    lanes = row.shape[1]
    sine, cosine = sine_cosine(phase)
    source[0] = SOURCE_GAIN * cosine
    source[1] = -SOURCE_GAIN * sine
    one, zero = jnp.ones((half_rows, lanes), BF16), jnp.zeros((half_rows, lanes), BF16)
    for half in range(2):
        row_ids = (lax.broadcasted_iota(jnp.int32, (half_rows, lanes), 0) + half * half_rows).astype(F32).astype(BF16)
        spread = []
        for group in range(groups):
            here = pl.ds(half * groups + group, 1)
            match = jnp.where(row_ids == tiled(row[here, :], half_rows), one, zero)
            parts = []
            for part in range(2):
                value = source[part, here, :]
                high = value.astype(BF16).astype(F32)
                parts += [match * tiled(high, half_rows), match * tiled(value - high, half_rows)]
            spread.append(jnp.concatenate(parts, 0))
        total = lax.dot_general(
            jnp.concatenate(spread, 1),
            hot[:, pl.ds(half * groups * lanes, groups * lanes)],
            (((1,), (1,)), ((), ())),
            preferred_element_type=F32,
        )
        own = pl.ds(half * half_rows, half_rows)
        for part in range(2):
            first = total[2 * part * half_rows : (2 * part + 1) * half_rows]
            second = total[(2 * part + 1) * half_rows : (2 * part + 2) * half_rows]
            field[part, own, :] += first + second


def diffract(field, out, mat):
    rows, cols = field.shape[1], field.shape[2]
    mat_high, mat_low = mat[0], mat[1]
    wide_high = jnp.concatenate([mat_high[:cols], mat_high[cols:]], 1)
    wide_low = jnp.concatenate([mat_low[:cols], mat_low[cols:]], 1)
    wide = jnp.concatenate([wide_high, wide_high, wide_low], 0)
    high, low = split(field[...].reshape(2 * rows, cols))
    turned = dot(jnp.concatenate([high, low, high], 1), wide)
    real = turned[:rows, :cols] - turned[rows:, cols:]
    imag = turned[:rows, cols:] + turned[rows:, :cols]
    high, low = split(jnp.concatenate([real, imag], 1))
    turned = dot(jnp.concatenate([mat_high, mat_high, mat_low], 1), jnp.concatenate([high, low, high], 0))
    out[0] = turned[:rows, :cols] - turned[rows:, cols:]
    out[1] = turned[:rows, cols:] + turned[rows:, :cols]


def kernel(
    blocks, wave, phase_hbm, energy_hbm, offset_hbm, row_hbm, col_hbm,
    wave_out, phase_out, energy_out,
    field, cells, pack, packed, leave, arrive, hot, sampled, source,
    phase_in, energy_in, offset_in, row_in, col_in, mat, load_sem,
    near_sem, far_send, far_recv, part_send, part_recv, own_sem, hand_sem,
    out_send, out_recv, out_own, out_last, leave_send, leave_recv, leave_last,
):
    t, r = lax.axis_index("tm"), lax.axis_index("row")
    other = 1 - r
    p = lax.rem(r + t, 2)
    first_after = lax.rem(t + 1, 2)
    after, before = lax.rem(t + 1, blocks), lax.rem(t + blocks - 1, blocks)
    slots = field.shape[0]
    half_rows = field.shape[2] // 2
    groups = cells.shape[2] // 2
    lanes = cells.shape[3]
    mine, theirs = pl.ds(r * half_rows, half_rows), pl.ds(other * half_rows, half_rows)
    inputs = (phase_in, energy_in, offset_in, row_in, col_in)
    sources = (phase_hbm, energy_hbm, offset_hbm, row_hbm, col_hbm)
    loads = [
        pltpu.make_async_copy(src, dst, load_sem.at[number])
        for number, (src, dst) in enumerate(zip(sources, inputs))
    ]
    for load in loads:
        load.start()

    def remote(src, dst, send, recv, where):
        return pltpu.make_async_remote_copy(
            src_ref=src, dst_ref=dst, send_sem=send, recv_sem=recv,
            device_id=where, device_id_type=pl.DeviceIdType.MESH,
        )

    def send_half(slot):
        item = slots * (1 - p) + slot - 1
        return remote(wave.at[item], field.at[slot, :, mine, :], near_sem.at[0, slot], near_sem.at[1, slot], (t, other))

    def receive_half(slot):
        return remote(wave.at[0], field.at[slot, :, theirs, :], near_sem.at[0, slot], near_sem.at[1, slot], (t, other))

    def send_last(half):
        return remote(
            wave.at[wave.shape[0] - 1], field.at[0, :, pl.ds(half * half_rows, half_rows), :],
            far_send.at[0], far_recv.at[half], (after, first_after),
        )

    def own_half(slot):
        return pltpu.make_async_copy(wave.at[slots * p + slot - 1], field.at[slot, :, mine, :], own_sem.at[slot])

    def send_part(pair):
        return remote(pack.at[pair], packed.at[pair], part_send.at[pair], part_recv.at[pair], (t, other))

    def pack_pair(pair):
        for slot in range(2 * pair, 2 * pair + 2):
            for number, ref in enumerate(inputs):
                kept = ref[pl.ds(slots * p + slot, 1), :].astype(F32)
                sent = ref[pl.ds(slots * (1 - p) + slot, 1), :].astype(F32)
                base = ((slot % 2) * 5 + number) * groups
                for group in range(groups):
                    piece = slice(group * lanes, (group + 1) * lanes)
                    cells[slot, number, pl.ds(r * groups + group, 1), :] = kept[:, piece]
                    pack[pair, pl.ds(base + group, 1), :] = sent[:, piece]

    def hand_over():
        return remote(
            cells.at[0], cells.at[slots], hand_sem.at[0], hand_sem.at[1],
            (jnp.where(p == 1, t, before), jnp.where(p == 1, other, r)),
        )

    def is_last(slot):
        return (p == 1) & (slot == slots - 1)

    def goal(slot):
        last = is_last(slot)
        return jnp.where(last, after, t), jnp.where(last, 0, slots * p + slot + 1)

    def send_out(slot):
        block, item = goal(slot)
        return remote(
            field.at[slot, :, theirs, :], wave_out.at[item], out_send.at[slot], out_recv.at[item], (block, other)
        )

    def send_out_last():
        return remote(field.at[slots - 1, :, mine, :], wave_out.at[0], out_last.at[0], out_recv.at[0], (after, r))

    def own_out(slot):
        return pltpu.make_async_copy(
            field.at[slot, :, mine, :], wave_out.at[slots * p + slot + 1], out_own.at[slot]
        )

    def send_leave(slot):
        block, item = goal(slot)
        return remote(
            leave.at[slot, other], arrive.at[item], leave_send.at[slot], leave_recv.at[item], (block, other)
        )

    def send_leave_last():
        return remote(leave.at[slots - 1, r], arrive.at[0], leave_last.at[0], leave_recv.at[0], (after, r))

    barrier = pltpu.get_barrier_semaphore()
    for peer in ((t, other), (after, 0), (after, 1), (before, 0), (before, 1)):
        pl.semaphore_signal(barrier, inc=1, device_id=peer, device_id_type=pl.DeviceIdType.MESH)

    pl.semaphore_wait(barrier, 5)

    @pl.when(t < blocks - 1)
    def _():
        send_last(r).start()

    @pl.when(p == 0)
    def _():
        send_half(0).start()

    @pl.when(p == 1)
    def _():
        own_half(0).start()

    for load in loads:
        load.wait()
    pack_pair(0)
    send_part(0).start()
    send_half(1).start()
    for pair in range(1, slots // 2):
        pack_pair(pair)
    for slot in range(1, slots):
        own_half(slot).start()

    fill_matrix(mat)

    @pl.when((t == 0) & (p == 0))
    def _():
        field[0] = jnp.zeros(field.shape[1:], F32)

    @pl.loop(0, 2 * slots)
    def _(turn):
        ending = turn == 2 * slots - 1
        second = ((turn > 0) & (turn % 2 == 0)) | ending
        slot = jnp.where(ending, slots - 1, jnp.where(turn % 2 == 0, jnp.maximum(turn // 2 - 1, 0), (turn + 1) // 2))
        cell = slot + second.astype(jnp.int32)

        @pl.when(jnp.logical_not(second))
        def _():
            pair, base = slot // 2, (slot % 2) * (5 * groups)

            @pl.when(slot % 2 == 0)
            def _():
                send_part(pair).wait_recv()

            for number in range(5):
                for group in range(groups):
                    cells[slot, number, pl.ds(other * groups + group, 1), :] = packed[
                        pair, pl.ds(base + number * groups + group, 1), :
                    ]

            @pl.when((p == 1) | (slot > 0))
            def _():
                own_half(slot).wait()
                receive_half(slot).wait_recv()

            @pl.when((p == 0) & (slot == 0) & (t > 0))
            def _():
                send_last(0).wait_recv()
                send_last(1).wait_recv()

            @pl.when((slot > 0) | (p == 0))
            def _():
                send_half(slot).wait_send()

            @pl.when((slot == 0) & (p == 1) & (t < blocks - 1))
            def _():
                send_last(r).wait_send()

            @pl.when(slot < slots - 2)
            def _():
                @pl.when(slot % 2 == 0)
                def _():
                    send_part(pair + 1).start()

                send_half(slot + 2).start()

        @pl.when(ending)
        def _():
            hand_over().wait_recv()

            @pl.when((p == 1) & (t == blocks - 1))
            def _():
                field[slots - 1] = jnp.zeros(field.shape[1:], F32)

        here = field.at[slot]
        push(here, cells.at[cell], hot, sampled)

        @pl.when(turn == 0)
        def _():
            hand_over().start()

        @pl.when(second)
        def _():
            for half in range(2):
                for number in range(2):
                    leave[slot, half, pl.ds(number * groups, groups), :] = cells[
                        cell, number, half * groups : (half + 1) * groups, :
                    ]
            send_leave(slot).start()

            @pl.when(is_last(slot))
            def _():
                send_leave_last().start()

            @pl.when(jnp.logical_not(is_last(slot)))
            def _():
                arrive[slots * p + slot + 1] = leave[slot, r]

        deposit(here, cells.at[cell], hot, source)

        diffract(here, here, mat)

        @pl.when(second)
        def _():
            send_out(slot).start()

            @pl.when(is_last(slot))
            def _():
                send_out_last().start()

            @pl.when(jnp.logical_not(is_last(slot)))
            def _():
                own_out(slot).start()

    def receive_leave(item):
        return remote(leave.at[0, 0], arrive.at[item], leave_send.at[0], leave_recv.at[item], (t, other))

    def receive_out(item):
        return remote(field.at[0, :, mine, :], wave_out.at[item], out_send.at[0], out_recv.at[item], (t, other))

    receive_leave(0).wait_recv()

    @pl.loop(0, slots)
    def _(slot):
        item = slots * (1 - p) + slot + 1

        @pl.when(item < 2 * slots)
        def _():
            receive_leave(item).wait_recv()

    for item in range(2 * slots):
        for group in range(groups):
            piece = pl.ds(group * lanes, lanes)
            phase_out[pl.ds(item, 1), piece] = arrive[item, pl.ds(group, 1), :]
            energy_out[pl.ds(item, 1), piece] = arrive[item, pl.ds(groups + group, 1), :]

    @pl.when((p == 0) & (t < blocks - 1))
    def _():
        send_last(r).wait_send()

    hand_over().wait_send()
    for pair in range(slots // 2):
        send_part(pair).wait_send()
    for slot in range(slots):
        send_leave(slot).wait_send()
        send_out(slot).wait_send()

        @pl.when(is_last(slot))
        def _():
            send_leave_last().wait_send()
            send_out_last().wait_send()

        @pl.when(jnp.logical_not(is_last(slot)))
        def _():
            own_out(slot).wait()

    receive_out(0).wait_recv()

    @pl.loop(0, slots)
    def _(slot):
        item = slots * (1 - p) + slot + 1

        @pl.when(item < 2 * slots)
        def _():
            receive_out(item).wait_recv()


def body(wavefront, particle_phase, particle_energy, row_offset, row_cell, col_cell):
    items, _, half_rows, cols = wavefront.shape
    slots, rows = items // 2, 2 * half_rows
    width = particle_phase.shape[1]
    groups = width // LANES
    operands = (wavefront, particle_phase, particle_energy, row_offset, row_cell, col_cell)
    vmem = pl.BlockSpec(memory_space=pltpu.VMEM)
    anywhere = pl.BlockSpec(memory_space=pl.ANY)
    dma = pltpu.SemaphoreType.DMA
    return pl.pallas_call(
        functools.partial(kernel, lax.axis_size("tm")),
        out_shape=(
            pltpu.VMEM(wavefront.shape, F32),
            pltpu.VMEM(particle_phase.shape, F32),
            pltpu.VMEM(particle_phase.shape, F32),
        ),
        in_specs=[pl.BlockSpec(memory_space=pltpu.HBM)] * 6,
        out_specs=(anywhere, vmem, vmem),
        scratch_shapes=[
            pltpu.VMEM((slots, 2, rows, cols), F32),
            pltpu.VMEM((slots + 1, 5, 2 * groups, LANES), F32),
            pltpu.VMEM((slots // 2, 10 * groups, LANES), F32),
            pltpu.VMEM((slots // 2, 10 * groups, LANES), F32),
            pltpu.VMEM((slots, 2, 2 * groups, LANES), F32),
            pltpu.VMEM((items, 2 * groups, LANES), F32),
            pltpu.VMEM((cols, 2 * width), BF16),
            pltpu.VMEM((2, 2 * groups, LANES), F32),
            pltpu.VMEM((2, 2 * groups, LANES), F32),
            *[pltpu.VMEM(particle_phase.shape, F32)] * 3,
            *[pltpu.VMEM(particle_phase.shape, jnp.int32)] * 2,
            pltpu.VMEM((2, 2 * cols, cols), BF16),
            dma((5,)),
            dma((2, slots)), dma((1,)), dma((2,)), dma((slots // 2,)), dma((slots // 2,)), dma((slots,)), dma((2,)),
            dma((slots,)), dma((items,)), dma((slots,)), dma((1,)), dma((slots,)), dma((items,)), dma((1,)),
        ],
        compiler_params=pltpu.CompilerParams(
            collective_id=0, has_side_effects=True, vmem_limit_bytes=48 * 1024 * 1024
        ),
        cost_estimate=pl.CostEstimate(flops=40 * 10**9, bytes_accessed=8 * 2**20, transcendentals=0),
    )(*(pltpu.with_memory_space_constraint(value, pltpu.HBM) for value in operands))


def solution(mesh):
    specs = (P("tm", None, "row", None),) + (P("tm", "row"),) * 5
    return jax.shard_map(body, mesh=mesh, in_specs=specs, out_specs=specs[:3], check_vma=False)
```

```python
import functools
import math

import jax
import jax.numpy as jnp
from jax import lax
from jax.experimental import pallas as pl
from jax.experimental.pallas import tpu as pltpu
from jax.sharding import PartitionSpec as P

PUSH_GAIN = 0.5
PHASE_ADVANCE = 1.0
SOURCE_GAIN = 1.0
LANES = 512
BF16 = jnp.bfloat16
F32 = jnp.float32


def split(value):
    high = value.astype(BF16)
    return high, (value - high.astype(F32)).astype(BF16)


def sine_cosine(angle):
    count = jnp.round(angle * (2.0 / math.pi))
    rest = angle - count * 1.5703125
    rest = rest - count * 4.837512969970703125e-4
    rest = rest - count * 7.54978995489188216e-8
    quadrant = count.astype(jnp.int32)
    square = rest * rest
    sine = rest + rest * square * (
        -1.6666654611e-1 + square * (8.3321608736e-3 + square * -1.9515295891e-4)
    )
    cosine = 1.0 + square * (
        -0.5 + square * (4.166664568298827e-2 + square * (-1.388731625493765e-3 + square * 2.443315711809948e-5))
    )
    swapped = (quadrant & 1) == 1
    sine_out = jnp.where(swapped, cosine, sine)
    cosine_out = jnp.where(swapped, sine, cosine)
    sine_out = jnp.where((quadrant & 2) == 2, -sine_out, sine_out)
    cosine_out = jnp.where(((quadrant + 1) & 2) == 2, -cosine_out, cosine_out)
    return sine_out, cosine_out


def tiled(row, count):
    tile = jnp.broadcast_to(row, (16, row.shape[1])).astype(BF16)
    return jnp.concatenate([tile] * (count // 16), 0)


def fill_matrix(mat):
    length = mat.shape[2]
    away = lax.broadcasted_iota(jnp.int32, (length, length), 0) - lax.broadcasted_iota(jnp.int32, (length, length), 1)
    turn = lax.rem(away * away, 2 * length).astype(F32)
    sine, cosine = sine_cosine((math.pi / length) * turn - math.pi / 4)
    for number, value in enumerate((cosine, sine)):
        for part, piece in enumerate(split(value * (1.0 / math.sqrt(length)))):
            mat[part, pl.ds(number * length, length), :] = piece


def dot(left, right):
    return jnp.dot(left, right, preferred_element_type=F32)


def push(field, cell, hot, sampled):
    phase, energy, offset, row, col = (cell.at[item] for item in range(5))
    rows, cols = field.shape[1], field.shape[2]
    half_rows = rows // 2
    window = half_rows + 16
    groups = row.shape[0] // 2
    lanes = row.shape[1]
    cells = lax.broadcasted_iota(jnp.int32, (cols, lanes), 0).astype(F32).astype(BF16)
    one, zero = jnp.ones((cols, lanes), BF16), jnp.zeros((cols, lanes), BF16)
    for half in range(2):
        start = 0 if half == 0 else half_rows - 16
        parts = jnp.concatenate(split(field[:, pl.ds(start, window), :].reshape(2 * window, cols)), 1)
        row_ids = (lax.broadcasted_iota(jnp.int32, (window, lanes), 0) + start).astype(F32)
        for group in range(groups):
            at = half * groups + group
            here = pl.ds(at, 1)
            one_hot = jnp.where(cells == tiled(col[here, :], cols), one, zero)
            hot[:, pl.ds(at * lanes, lanes)] = one_hot
            mixed = dot(parts, jnp.concatenate([one_hot, one_hot], 0))
            place = row[here, :]
            f = offset[here, :]
            weight = jnp.where(row_ids == place - 1.0, 0.5 * (0.5 - f) * (0.5 - f), 0.0)
            weight = jnp.where(row_ids == place, 0.75 - f * f, weight)
            weight = jnp.where(row_ids == place + 1.0, 0.5 * (0.5 + f) * (0.5 + f), weight)
            sampled[0, here, :] = jnp.sum(weight * mixed[:window], axis=0, keepdims=True)
            sampled[1, here, :] = jnp.sum(weight * mixed[window:], axis=0, keepdims=True)
    sine, cosine = sine_cosine(phase[...])
    energy[...] = energy[...] - PUSH_GAIN * (sampled[0] * cosine - sampled[1] * sine)
    phase[...] = phase[...] + PHASE_ADVANCE * energy[...]


def deposit(field, cell, hot, source):
    phase, row = cell[0], cell.at[3]
    rows = field.shape[1]
    half_rows = rows // 2
    groups = row.shape[0] // 2
    lanes = row.shape[1]
    sine, cosine = sine_cosine(phase)
    source[0] = SOURCE_GAIN * cosine
    source[1] = -SOURCE_GAIN * sine
    one, zero = jnp.ones((half_rows, lanes), BF16), jnp.zeros((half_rows, lanes), BF16)
    for half in range(2):
        row_ids = (lax.broadcasted_iota(jnp.int32, (half_rows, lanes), 0) + half * half_rows).astype(F32).astype(BF16)
        spread = []
        for group in range(groups):
            here = pl.ds(half * groups + group, 1)
            match = jnp.where(row_ids == tiled(row[here, :], half_rows), one, zero)
            parts = []
            for part in range(2):
                value = source[part, here, :]
                high = value.astype(BF16).astype(F32)
                parts += [match * tiled(high, half_rows), match * tiled(value - high, half_rows)]
            spread.append(jnp.concatenate(parts, 0))
        total = lax.dot_general(
            jnp.concatenate(spread, 1),
            hot[:, pl.ds(half * groups * lanes, groups * lanes)],
            (((1,), (1,)), ((), ())),
            preferred_element_type=F32,
        )
        own = pl.ds(half * half_rows, half_rows)
        for part in range(2):
            first = total[2 * part * half_rows : (2 * part + 1) * half_rows]
            second = total[(2 * part + 1) * half_rows : (2 * part + 2) * half_rows]
            field[part, own, :] += first + second


def diffract(field, out, mat):
    rows, cols = field.shape[1], field.shape[2]
    mat_high, mat_low = mat[0], mat[1]
    wide_high = jnp.concatenate([mat_high[:cols], mat_high[cols:]], 1)
    wide_low = jnp.concatenate([mat_low[:cols], mat_low[cols:]], 1)
    wide = jnp.concatenate([wide_high, wide_high, wide_low], 0)
    high, low = split(field[...].reshape(2 * rows, cols))
    turned = dot(jnp.concatenate([high, low, high], 1), wide)
    real = turned[:rows, :cols] - turned[rows:, cols:]
    imag = turned[:rows, cols:] + turned[rows:, :cols]
    high, low = split(jnp.concatenate([real, imag], 1))
    turned = dot(jnp.concatenate([mat_high, mat_high, mat_low], 1), jnp.concatenate([high, low, high], 0))
    out[0] = turned[:rows, :cols] - turned[rows:, cols:]
    out[1] = turned[:rows, cols:] + turned[rows:, :cols]


def kernel(
    blocks, wave, phase_hbm, energy_hbm, offset_hbm, row_hbm, col_hbm,
    wave_out, phase_out, energy_out,
    field, cells, pack, packed, leave, arrive, hot, sampled, source,
    phase_in, energy_in, offset_in, row_in, col_in, mat, load_sem,
    near_sem, far_send, far_recv, part_send, part_recv, own_sem, hand_sem,
    out_send, out_recv, out_own, out_last, leave_send, leave_recv, leave_last,
):
    t, r = lax.axis_index("tm"), lax.axis_index("row")
    other = 1 - r
    p = lax.rem(r + t, 2)
    first_after = lax.rem(t + 1, 2)
    after, before = lax.rem(t + 1, blocks), lax.rem(t + blocks - 1, blocks)
    slots = field.shape[0]
    half_rows = field.shape[2] // 2
    groups = cells.shape[2] // 2
    lanes = cells.shape[3]
    mine, theirs = pl.ds(r * half_rows, half_rows), pl.ds(other * half_rows, half_rows)
    inputs = (phase_in, energy_in, offset_in, row_in, col_in)
    sources = (phase_hbm, energy_hbm, offset_hbm, row_hbm, col_hbm)
    loads = [
        pltpu.make_async_copy(src, dst, load_sem.at[number])
        for number, (src, dst) in enumerate(zip(sources, inputs))
    ]
    for load in loads:
        load.start()

    def remote(src, dst, send, recv, where):
        return pltpu.make_async_remote_copy(
            src_ref=src, dst_ref=dst, send_sem=send, recv_sem=recv,
            device_id=where, device_id_type=pl.DeviceIdType.MESH,
        )

    def send_half(slot):
        item = slots * (1 - p) + slot - 1
        return remote(wave.at[item], field.at[slot, :, mine, :], near_sem.at[0, slot], near_sem.at[1, slot], (t, other))

    def receive_half(slot):
        return remote(wave.at[0], field.at[slot, :, theirs, :], near_sem.at[0, slot], near_sem.at[1, slot], (t, other))

    def send_last(half):
        return remote(
            wave.at[wave.shape[0] - 1], field.at[0, :, pl.ds(half * half_rows, half_rows), :],
            far_send.at[0], far_recv.at[half], (after, first_after),
        )

    def own_half(slot):
        return pltpu.make_async_copy(wave.at[slots * p + slot - 1], field.at[slot, :, mine, :], own_sem.at[slot])

    def send_part(pair):
        return remote(pack.at[pair], packed.at[pair], part_send.at[pair], part_recv.at[pair], (t, other))

    def pack_pair(pair):
        for slot in range(2 * pair, 2 * pair + 2):
            for number, ref in enumerate(inputs):
                kept = ref[pl.ds(slots * p + slot, 1), :].astype(F32)
                sent = ref[pl.ds(slots * (1 - p) + slot, 1), :].astype(F32)
                base = ((slot % 2) * 5 + number) * groups
                for group in range(groups):
                    piece = slice(group * lanes, (group + 1) * lanes)
                    cells[slot, number, pl.ds(r * groups + group, 1), :] = kept[:, piece]
                    pack[pair, pl.ds(base + group, 1), :] = sent[:, piece]

    def hand_over():
        return remote(
            cells.at[0], cells.at[slots], hand_sem.at[0], hand_sem.at[1],
            (jnp.where(p == 1, t, before), jnp.where(p == 1, other, r)),
        )

    def is_last(slot):
        return (p == 1) & (slot == slots - 1)

    def goal(slot):
        last = is_last(slot)
        return jnp.where(last, after, t), jnp.where(last, 0, slots * p + slot + 1)

    def send_out(slot):
        block, item = goal(slot)
        return remote(
            field.at[slot, :, theirs, :], wave_out.at[item], out_send.at[slot], out_recv.at[item], (block, other)
        )

    def send_out_last():
        return remote(field.at[slots - 1, :, mine, :], wave_out.at[0], out_last.at[0], out_recv.at[0], (after, r))

    def own_out(slot):
        return pltpu.make_async_copy(
            field.at[slot, :, mine, :], wave_out.at[slots * p + slot + 1], out_own.at[slot]
        )

    def send_leave(slot):
        block, item = goal(slot)
        return remote(
            leave.at[slot, other], arrive.at[item], leave_send.at[slot], leave_recv.at[item], (block, other)
        )

    def send_leave_last():
        return remote(leave.at[slots - 1, r], arrive.at[0], leave_last.at[0], leave_recv.at[0], (after, r))

    barrier = pltpu.get_barrier_semaphore()
    for peer in ((t, other), (after, 0), (after, 1), (before, 0), (before, 1)):
        pl.semaphore_signal(barrier, inc=1, device_id=peer, device_id_type=pl.DeviceIdType.MESH)

    pl.semaphore_wait(barrier, 5)

    @pl.when(t < blocks - 1)
    def _():
        send_last(r).start()

    @pl.when(p == 0)
    def _():
        send_half(0).start()

    @pl.when(p == 1)
    def _():
        own_half(0).start()

    for load in loads:
        load.wait()
    pack_pair(0)
    send_part(0).start()
    send_half(1).start()
    for pair in range(1, slots // 2):
        pack_pair(pair)
    for slot in range(1, slots):
        own_half(slot).start()

    fill_matrix(mat)

    @pl.when((t == 0) & (p == 0))
    def _():
        field[0] = jnp.zeros(field.shape[1:], F32)

    @pl.loop(0, 2 * slots)
    def _(turn):
        ending = turn == 2 * slots - 2
        final = turn == 2 * slots - 1
        second = ((turn > 0) & (turn % 2 == 0)) | final
        slot = jnp.where(turn % 2 == 0, jnp.maximum(turn // 2 - 1, 0), (turn + 1) // 2)
        slot = jnp.where(ending, slots - 1, jnp.where(final, slots - 2, slot))
        cell = slot + second.astype(jnp.int32)

        @pl.when(jnp.logical_not(second))
        def _():
            pair, base = slot // 2, (slot % 2) * (5 * groups)

            @pl.when(slot % 2 == 0)
            def _():
                send_part(pair).wait_recv()

            for number in range(5):
                for group in range(groups):
                    cells[slot, number, pl.ds(other * groups + group, 1), :] = packed[
                        pair, pl.ds(base + number * groups + group, 1), :
                    ]

            @pl.when((p == 1) | (slot > 0))
            def _():
                own_half(slot).wait()
                receive_half(slot).wait_recv()

            @pl.when((p == 0) & (slot == 0) & (t > 0))
            def _():
                send_last(0).wait_recv()
                send_last(1).wait_recv()

            @pl.when((slot > 0) | (p == 0))
            def _():
                send_half(slot).wait_send()

            @pl.when((slot == 0) & (p == 1) & (t < blocks - 1))
            def _():
                send_last(r).wait_send()

            @pl.when(slot < slots - 2)
            def _():
                @pl.when(slot % 2 == 0)
                def _():
                    send_part(pair + 1).start()

                send_half(slot + 2).start()

        @pl.when(ending)
        def _():
            hand_over().wait_recv()

            @pl.when((p == 1) & (t == blocks - 1))
            def _():
                field[slots - 1] = jnp.zeros(field.shape[1:], F32)

        here = field.at[slot]
        push(here, cells.at[cell], hot, sampled)

        @pl.when(turn == 0)
        def _():
            hand_over().start()

        @pl.when(second)
        def _():
            for half in range(2):
                for number in range(2):
                    leave[slot, half, pl.ds(number * groups, groups), :] = cells[
                        cell, number, half * groups : (half + 1) * groups, :
                    ]
            send_leave(slot).start()

            @pl.when(is_last(slot))
            def _():
                send_leave_last().start()

            @pl.when(jnp.logical_not(is_last(slot)))
            def _():
                arrive[slots * p + slot + 1] = leave[slot, r]

        deposit(here, cells.at[cell], hot, source)

        diffract(here, here, mat)

        @pl.when(second)
        def _():
            send_out(slot).start()

            @pl.when(is_last(slot))
            def _():
                send_out_last().start()

            @pl.when(jnp.logical_not(is_last(slot)))
            def _():
                own_out(slot).start()

    def receive_leave(item):
        return remote(leave.at[0, 0], arrive.at[item], leave_send.at[0], leave_recv.at[item], (t, other))

    def receive_out(item):
        return remote(field.at[0, :, mine, :], wave_out.at[item], out_send.at[0], out_recv.at[item], (t, other))

    receive_leave(0).wait_recv()

    @pl.loop(0, slots)
    def _(slot):
        item = slots * (1 - p) + slot + 1

        @pl.when(item < 2 * slots)
        def _():
            receive_leave(item).wait_recv()

    for item in range(2 * slots):
        for group in range(groups):
            piece = pl.ds(group * lanes, lanes)
            phase_out[pl.ds(item, 1), piece] = arrive[item, pl.ds(group, 1), :]
            energy_out[pl.ds(item, 1), piece] = arrive[item, pl.ds(groups + group, 1), :]

    @pl.when((p == 0) & (t < blocks - 1))
    def _():
        send_last(r).wait_send()

    hand_over().wait_send()
    for pair in range(slots // 2):
        send_part(pair).wait_send()
    for slot in range(slots):
        send_leave(slot).wait_send()
        send_out(slot).wait_send()

        @pl.when(is_last(slot))
        def _():
            send_leave_last().wait_send()
            send_out_last().wait_send()

        @pl.when(jnp.logical_not(is_last(slot)))
        def _():
            own_out(slot).wait()

    receive_out(0).wait_recv()

    @pl.loop(0, slots)
    def _(slot):
        item = slots * (1 - p) + slot + 1

        @pl.when(item < 2 * slots)
        def _():
            receive_out(item).wait_recv()


def store_kernel(*refs):
    sem = refs[-1]
    copies = [pltpu.make_async_copy(refs[i], refs[3 + i], sem.at[i]) for i in range(3)]
    for copy in copies:
        copy.start()
    for copy in copies:
        copy.wait()


def body(wavefront, particle_phase, particle_energy, row_offset, row_cell, col_cell):
    items, _, half_rows, cols = wavefront.shape
    slots, rows = items // 2, 2 * half_rows
    width = particle_phase.shape[1]
    groups = width // LANES
    operands = (wavefront, particle_phase, particle_energy, row_offset, row_cell, col_cell)
    vmem = pl.BlockSpec(memory_space=pltpu.VMEM)
    anywhere = pl.BlockSpec(memory_space=pl.ANY)
    dma = pltpu.SemaphoreType.DMA
    results = pl.pallas_call(
        functools.partial(kernel, lax.axis_size("tm")),
        out_shape=(
            pltpu.VMEM(wavefront.shape, F32),
            pltpu.VMEM(particle_phase.shape, F32),
            pltpu.VMEM(particle_phase.shape, F32),
        ),
        in_specs=[pl.BlockSpec(memory_space=pltpu.HBM)] * 6,
        out_specs=(anywhere, vmem, vmem),
        scratch_shapes=[
            pltpu.VMEM((slots, 2, rows, cols), F32),
            pltpu.VMEM((slots + 1, 5, 2 * groups, LANES), F32),
            pltpu.VMEM((slots // 2, 10 * groups, LANES), F32),
            pltpu.VMEM((slots // 2, 10 * groups, LANES), F32),
            pltpu.VMEM((slots, 2, 2 * groups, LANES), F32),
            pltpu.VMEM((items, 2 * groups, LANES), F32),
            pltpu.VMEM((cols, 2 * width), BF16),
            pltpu.VMEM((2, 2 * groups, LANES), F32),
            pltpu.VMEM((2, 2 * groups, LANES), F32),
            *[pltpu.VMEM(particle_phase.shape, F32)] * 3,
            *[pltpu.VMEM(particle_phase.shape, jnp.int32)] * 2,
            pltpu.VMEM((2, 2 * cols, cols), BF16),
            dma((5,)),
            dma((2, slots)), dma((1,)), dma((2,)), dma((slots // 2,)), dma((slots // 2,)), dma((slots,)), dma((2,)),
            dma((slots,)), dma((items,)), dma((slots,)), dma((1,)), dma((slots,)), dma((items,)), dma((1,)),
        ],
        compiler_params=pltpu.CompilerParams(
            collective_id=0, has_side_effects=True, vmem_limit_bytes=48 * 1024 * 1024
        ),
        cost_estimate=pl.CostEstimate(flops=40 * 10**9, bytes_accessed=8 * 2**20, transcendentals=0),
    )(*(pltpu.with_memory_space_constraint(value, pltpu.HBM) for value in operands))
    return pl.pallas_call(
        store_kernel,
        out_shape=tuple(pltpu.HBM(value.shape, F32) for value in results),
        in_specs=[anywhere] * 3,
        out_specs=(anywhere,) * 3,
        scratch_shapes=[dma((3,))],
        cost_estimate=pl.CostEstimate(flops=0, bytes_accessed=4 * 2**20, transcendentals=0),
    )(*(pltpu.with_memory_space_constraint(value, pltpu.VMEM) for value in results))


def solution(mesh):
    specs = (P("tm", None, "row", None),) + (P("tm", "row"),) * 5
    return jax.shard_map(body, mesh=mesh, in_specs=specs, out_specs=specs[:3], check_vma=False)
```

```python
import functools
import math

import jax
import jax.numpy as jnp
from jax import lax
from jax.experimental import pallas as pl
from jax.experimental.pallas import tpu as pltpu
from jax.sharding import PartitionSpec as P

PUSH_GAIN = 0.5
PHASE_ADVANCE = 1.0
SOURCE_GAIN = 1.0
LANES = 512
BF16 = jnp.bfloat16
F32 = jnp.float32


def split(value):
    high = value.astype(BF16)
    return high, (value - high.astype(F32)).astype(BF16)


def sine_cosine(angle):
    count = jnp.round(angle * (2.0 / math.pi))
    rest = angle - count * 1.5703125
    rest = rest - count * 4.837512969970703125e-4
    rest = rest - count * 7.54978995489188216e-8
    quadrant = count.astype(jnp.int32)
    square = rest * rest
    sine = rest + rest * square * (
        -1.6666654611e-1 + square * (8.3321608736e-3 + square * -1.9515295891e-4)
    )
    cosine = 1.0 + square * (
        -0.5 + square * (4.166664568298827e-2 + square * (-1.388731625493765e-3 + square * 2.443315711809948e-5))
    )
    swapped = (quadrant & 1) == 1
    sine_out = jnp.where(swapped, cosine, sine)
    cosine_out = jnp.where(swapped, sine, cosine)
    sine_out = jnp.where((quadrant & 2) == 2, -sine_out, sine_out)
    cosine_out = jnp.where(((quadrant + 1) & 2) == 2, -cosine_out, cosine_out)
    return sine_out, cosine_out


def tiled(row, count):
    tile = jnp.broadcast_to(row, (16, row.shape[1])).astype(BF16)
    return jnp.concatenate([tile] * (count // 16), 0)


def fill_matrix(mat):
    length = mat.shape[2]
    away = lax.broadcasted_iota(jnp.int32, (length, length), 0) - lax.broadcasted_iota(jnp.int32, (length, length), 1)
    turn = lax.rem(away * away, 2 * length).astype(F32)
    sine, cosine = sine_cosine((math.pi / length) * turn - math.pi / 4)
    for number, value in enumerate((cosine, sine)):
        for part, piece in enumerate(split(value * (1.0 / math.sqrt(length)))):
            mat[part, pl.ds(number * length, length), :] = piece


def dot(left, right):
    return jnp.dot(left, right, preferred_element_type=F32)


def push(field, cell, hot, sampled):
    phase, energy, offset, row, col = (cell.at[item] for item in range(5))
    rows, cols = field.shape[1], field.shape[2]
    half_rows = rows // 2
    window = half_rows + 16
    groups = row.shape[0] // 2
    lanes = row.shape[1]
    cells = lax.broadcasted_iota(jnp.int32, (cols, lanes), 0).astype(F32).astype(BF16)
    one, zero = jnp.ones((cols, lanes), BF16), jnp.zeros((cols, lanes), BF16)
    for half in range(2):
        start = 0 if half == 0 else half_rows - 16
        parts = jnp.concatenate(split(field[:, pl.ds(start, window), :].reshape(2 * window, cols)), 1)
        row_ids = (lax.broadcasted_iota(jnp.int32, (window, lanes), 0) + start).astype(F32)
        for group in range(groups):
            at = half * groups + group
            here = pl.ds(at, 1)
            one_hot = jnp.where(cells == tiled(col[here, :], cols), one, zero)
            hot[:, pl.ds(at * lanes, lanes)] = one_hot
            mixed = dot(parts, jnp.concatenate([one_hot, one_hot], 0))
            place = row[here, :]
            f = offset[here, :]
            weight = jnp.where(row_ids == place - 1.0, 0.5 * (0.5 - f) * (0.5 - f), 0.0)
            weight = jnp.where(row_ids == place, 0.75 - f * f, weight)
            weight = jnp.where(row_ids == place + 1.0, 0.5 * (0.5 + f) * (0.5 + f), weight)
            sampled[0, here, :] = jnp.sum(weight * mixed[:window], axis=0, keepdims=True)
            sampled[1, here, :] = jnp.sum(weight * mixed[window:], axis=0, keepdims=True)
    sine, cosine = sine_cosine(phase[...])
    energy[...] = energy[...] - PUSH_GAIN * (sampled[0] * cosine - sampled[1] * sine)
    phase[...] = phase[...] + PHASE_ADVANCE * energy[...]


def deposit(field, cell, hot, source):
    phase, row = cell[0], cell.at[3]
    rows = field.shape[1]
    half_rows = rows // 2
    groups = row.shape[0] // 2
    lanes = row.shape[1]
    sine, cosine = sine_cosine(phase)
    source[0] = SOURCE_GAIN * cosine
    source[1] = -SOURCE_GAIN * sine
    one, zero = jnp.ones((half_rows, lanes), BF16), jnp.zeros((half_rows, lanes), BF16)
    for half in range(2):
        row_ids = (lax.broadcasted_iota(jnp.int32, (half_rows, lanes), 0) + half * half_rows).astype(F32).astype(BF16)
        spread = []
        for group in range(groups):
            here = pl.ds(half * groups + group, 1)
            match = jnp.where(row_ids == tiled(row[here, :], half_rows), one, zero)
            parts = []
            for part in range(2):
                value = source[part, here, :]
                high = value.astype(BF16).astype(F32)
                parts += [match * tiled(high, half_rows), match * tiled(value - high, half_rows)]
            spread.append(jnp.concatenate(parts, 0))
        total = lax.dot_general(
            jnp.concatenate(spread, 1),
            hot[:, pl.ds(half * groups * lanes, groups * lanes)],
            (((1,), (1,)), ((), ())),
            preferred_element_type=F32,
        )
        own = pl.ds(half * half_rows, half_rows)
        for part in range(2):
            first = total[2 * part * half_rows : (2 * part + 1) * half_rows]
            second = total[(2 * part + 1) * half_rows : (2 * part + 2) * half_rows]
            field[part, own, :] += first + second


def diffract(field, out, mat):
    rows, cols = field.shape[1], field.shape[2]
    mat_high, mat_low = mat[0], mat[1]
    wide_high = jnp.concatenate([mat_high[:cols], mat_high[cols:]], 1)
    wide_low = jnp.concatenate([mat_low[:cols], mat_low[cols:]], 1)
    wide = jnp.concatenate([wide_high, wide_high, wide_low], 0)
    high, low = split(field[...].reshape(2 * rows, cols))
    turned = dot(jnp.concatenate([high, low, high], 1), wide)
    real = turned[:rows, :cols] - turned[rows:, cols:]
    imag = turned[:rows, cols:] + turned[rows:, :cols]
    high, low = split(jnp.concatenate([real, imag], 1))
    turned = dot(jnp.concatenate([mat_high, mat_high, mat_low], 1), jnp.concatenate([high, low, high], 0))
    out[0] = turned[:rows, :cols] - turned[rows:, cols:]
    out[1] = turned[:rows, cols:] + turned[rows:, :cols]


def kernel(
    blocks, wave, phase_hbm, energy_hbm, offset_hbm, row_hbm, col_hbm,
    wave_out, phase_out, energy_out,
    field, cells, pack, packed, leave, arrive, hot, sampled, source,
    phase_in, energy_in, offset_in, row_in, col_in, mat, load_sem,
    near_sem, far_send, far_recv, part_send, part_recv, own_sem, hand_sem,
    out_send, out_recv, out_own, out_last, leave_send, leave_recv, leave_last,
):
    t, r = lax.axis_index("tm"), lax.axis_index("row")
    other = 1 - r
    p = lax.rem(r + t, 2)
    first_after = lax.rem(t + 1, 2)
    after, before = lax.rem(t + 1, blocks), lax.rem(t + blocks - 1, blocks)
    slots = field.shape[0]
    half_rows = field.shape[2] // 2
    groups = cells.shape[2] // 2
    lanes = cells.shape[3]
    mine, theirs = pl.ds(r * half_rows, half_rows), pl.ds(other * half_rows, half_rows)
    inputs = (phase_in, energy_in, offset_in, row_in, col_in)
    sources = (phase_hbm, energy_hbm, offset_hbm, row_hbm, col_hbm)
    loads = [
        pltpu.make_async_copy(src, dst, load_sem.at[number])
        for number, (src, dst) in enumerate(zip(sources, inputs))
    ]
    for load in loads:
        load.start()

    def remote(src, dst, send, recv, where):
        return pltpu.make_async_remote_copy(
            src_ref=src, dst_ref=dst, send_sem=send, recv_sem=recv,
            device_id=where, device_id_type=pl.DeviceIdType.MESH,
        )

    def send_half(slot):
        item = slots * (1 - p) + slot - 1
        return remote(wave.at[item], field.at[slot, :, mine, :], near_sem.at[0, slot], near_sem.at[1, slot], (t, other))

    def receive_half(slot):
        return remote(wave.at[0], field.at[slot, :, theirs, :], near_sem.at[0, slot], near_sem.at[1, slot], (t, other))

    def send_last(half):
        return remote(
            wave.at[wave.shape[0] - 1], field.at[0, :, pl.ds(half * half_rows, half_rows), :],
            far_send.at[0], far_recv.at[half], (after, first_after),
        )

    def own_half(slot):
        return pltpu.make_async_copy(wave.at[slots * p + slot - 1], field.at[slot, :, mine, :], own_sem.at[slot])

    def send_part(pair):
        return remote(pack.at[pair], packed.at[pair], part_send.at[pair], part_recv.at[pair], (t, other))

    def pack_pair(pair):
        for slot in range(2 * pair, 2 * pair + 2):
            for number, ref in enumerate(inputs):
                kept = ref[pl.ds(slots * p + slot, 1), :].astype(F32)
                sent = ref[pl.ds(slots * (1 - p) + slot, 1), :].astype(F32)
                base = ((slot % 2) * 5 + number) * groups
                for group in range(groups):
                    piece = slice(group * lanes, (group + 1) * lanes)
                    cells[slot, number, pl.ds(r * groups + group, 1), :] = kept[:, piece]
                    pack[pair, pl.ds(base + group, 1), :] = sent[:, piece]

    def hand_over():
        return remote(
            cells.at[0], cells.at[slots], hand_sem.at[0], hand_sem.at[1],
            (jnp.where(p == 1, t, before), jnp.where(p == 1, other, r)),
        )

    def is_last(slot):
        return (p == 1) & (slot == slots - 1)

    def goal(slot):
        last = is_last(slot)
        return jnp.where(last, after, t), jnp.where(last, 0, slots * p + slot + 1)

    def send_out(slot):
        block, item = goal(slot)
        return remote(
            field.at[slot, :, theirs, :], wave_out.at[item], out_send.at[slot], out_recv.at[item], (block, other)
        )

    def send_out_last():
        return remote(field.at[slots - 1, :, mine, :], wave_out.at[0], out_last.at[0], out_recv.at[0], (after, r))

    def own_out(slot):
        return pltpu.make_async_copy(
            field.at[slot, :, mine, :], wave_out.at[slots * p + slot + 1], out_own.at[slot]
        )

    def send_leave(slot):
        block, item = goal(slot)
        return remote(
            leave.at[slot, other], arrive.at[item], leave_send.at[slot], leave_recv.at[item], (block, other)
        )

    def send_leave_last():
        return remote(leave.at[slots - 1, r], arrive.at[0], leave_last.at[0], leave_recv.at[0], (after, r))

    barrier = pltpu.get_barrier_semaphore()
    for peer in ((t, other), (after, 0), (after, 1), (before, 0), (before, 1)):
        pl.semaphore_signal(barrier, inc=1, device_id=peer, device_id_type=pl.DeviceIdType.MESH)

    pl.semaphore_wait(barrier, 5)

    @pl.when(t < blocks - 1)
    def _():
        send_last(r).start()

    @pl.when(p == 0)
    def _():
        send_half(0).start()

    @pl.when(p == 1)
    def _():
        own_half(0).start()

    for load in loads:
        load.wait()
    pack_pair(0)
    send_part(0).start()
    send_half(1).start()
    for pair in range(1, slots // 2):
        pack_pair(pair)
        send_part(pair).start()
        send_half(2 * pair).start()
        send_half(2 * pair + 1).start()
    for slot in range(1, slots):
        own_half(slot).start()

    fill_matrix(mat)

    @pl.when((t == 0) & (p == 0))
    def _():
        field[0] = jnp.zeros(field.shape[1:], F32)

    @pl.loop(0, 2 * slots)
    def _(turn):
        ending = turn == 2 * slots - 2
        final = turn == 2 * slots - 1
        second = ((turn > 0) & (turn % 2 == 0)) | final
        slot = jnp.where(turn % 2 == 0, jnp.maximum(turn // 2 - 1, 0), (turn + 1) // 2)
        slot = jnp.where(ending, slots - 1, jnp.where(final, slots - 2, slot))
        cell = slot + second.astype(jnp.int32)

        @pl.when(jnp.logical_not(second))
        def _():
            pair, base = slot // 2, (slot % 2) * (5 * groups)

            @pl.when(slot % 2 == 0)
            def _():
                send_part(pair).wait_recv()

            for number in range(5):
                for group in range(groups):
                    cells[slot, number, pl.ds(other * groups + group, 1), :] = packed[
                        pair, pl.ds(base + number * groups + group, 1), :
                    ]

            @pl.when((p == 1) | (slot > 0))
            def _():
                own_half(slot).wait()
                receive_half(slot).wait_recv()

            @pl.when((p == 0) & (slot == 0) & (t > 0))
            def _():
                send_last(0).wait_recv()
                send_last(1).wait_recv()


        @pl.when(ending)
        def _():
            hand_over().wait_recv()

            @pl.when((p == 1) & (t == blocks - 1))
            def _():
                field[slots - 1] = jnp.zeros(field.shape[1:], F32)

        here = field.at[slot]
        push(here, cells.at[cell], hot, sampled)

        @pl.when(turn == 0)
        def _():
            hand_over().start()

        @pl.when(second)
        def _():
            for half in range(2):
                for number in range(2):
                    leave[slot, half, pl.ds(number * groups, groups), :] = cells[
                        cell, number, half * groups : (half + 1) * groups, :
                    ]
            send_leave(slot).start()

            @pl.when(is_last(slot))
            def _():
                send_leave_last().start()

            @pl.when(jnp.logical_not(is_last(slot)))
            def _():
                arrive[slots * p + slot + 1] = leave[slot, r]

        deposit(here, cells.at[cell], hot, source)

        diffract(here, here, mat)

        @pl.when(second)
        def _():
            send_out(slot).start()

            @pl.when(is_last(slot))
            def _():
                send_out_last().start()

            @pl.when(jnp.logical_not(is_last(slot)))
            def _():
                own_out(slot).start()

    def receive_leave(item):
        return remote(leave.at[0, 0], arrive.at[item], leave_send.at[0], leave_recv.at[item], (t, other))

    def receive_out(item):
        return remote(field.at[0, :, mine, :], wave_out.at[item], out_send.at[0], out_recv.at[item], (t, other))

    receive_leave(0).wait_recv()

    @pl.loop(0, slots)
    def _(slot):
        item = slots * (1 - p) + slot + 1

        @pl.when(item < 2 * slots)
        def _():
            receive_leave(item).wait_recv()

    for item in range(2 * slots):
        for group in range(groups):
            piece = pl.ds(group * lanes, lanes)
            phase_out[pl.ds(item, 1), piece] = arrive[item, pl.ds(group, 1), :]
            energy_out[pl.ds(item, 1), piece] = arrive[item, pl.ds(groups + group, 1), :]

    @pl.when(t < blocks - 1)
    def _():
        send_last(r).wait_send()

    @pl.when(p == 0)
    def _():
        send_half(0).wait_send()

    hand_over().wait_send()
    for pair in range(slots // 2):
        send_part(pair).wait_send()
    for slot in range(slots):
        if slot > 0:
            send_half(slot).wait_send()
        send_leave(slot).wait_send()
        send_out(slot).wait_send()

        @pl.when(is_last(slot))
        def _():
            send_leave_last().wait_send()
            send_out_last().wait_send()

        @pl.when(jnp.logical_not(is_last(slot)))
        def _():
            own_out(slot).wait()

    receive_out(0).wait_recv()

    @pl.loop(0, slots)
    def _(slot):
        item = slots * (1 - p) + slot + 1

        @pl.when(item < 2 * slots)
        def _():
            receive_out(item).wait_recv()


def store_kernel(*refs):
    sem = refs[-1]
    copies = [pltpu.make_async_copy(refs[i], refs[3 + i], sem.at[i]) for i in range(3)]
    for copy in copies:
        copy.start()
    for copy in copies:
        copy.wait()


def body(wavefront, particle_phase, particle_energy, row_offset, row_cell, col_cell):
    items, _, half_rows, cols = wavefront.shape
    slots, rows = items // 2, 2 * half_rows
    width = particle_phase.shape[1]
    groups = width // LANES
    operands = (wavefront, particle_phase, particle_energy, row_offset, row_cell, col_cell)
    vmem = pl.BlockSpec(memory_space=pltpu.VMEM)
    anywhere = pl.BlockSpec(memory_space=pl.ANY)
    dma = pltpu.SemaphoreType.DMA
    results = pl.pallas_call(
        functools.partial(kernel, lax.axis_size("tm")),
        out_shape=(
            pltpu.VMEM(wavefront.shape, F32),
            pltpu.VMEM(particle_phase.shape, F32),
            pltpu.VMEM(particle_phase.shape, F32),
        ),
        in_specs=[pl.BlockSpec(memory_space=pltpu.HBM)] * 6,
        out_specs=(anywhere, vmem, vmem),
        scratch_shapes=[
            pltpu.VMEM((slots, 2, rows, cols), F32),
            pltpu.VMEM((slots + 1, 5, 2 * groups, LANES), F32),
            pltpu.VMEM((slots // 2, 10 * groups, LANES), F32),
            pltpu.VMEM((slots // 2, 10 * groups, LANES), F32),
            pltpu.VMEM((slots, 2, 2 * groups, LANES), F32),
            pltpu.VMEM((items, 2 * groups, LANES), F32),
            pltpu.VMEM((cols, 2 * width), BF16),
            pltpu.VMEM((2, 2 * groups, LANES), F32),
            pltpu.VMEM((2, 2 * groups, LANES), F32),
            *[pltpu.VMEM(particle_phase.shape, F32)] * 3,
            *[pltpu.VMEM(particle_phase.shape, jnp.int32)] * 2,
            pltpu.VMEM((2, 2 * cols, cols), BF16),
            dma((5,)),
            dma((2, slots)), dma((1,)), dma((2,)), dma((slots // 2,)), dma((slots // 2,)), dma((slots,)), dma((2,)),
            dma((slots,)), dma((items,)), dma((slots,)), dma((1,)), dma((slots,)), dma((items,)), dma((1,)),
        ],
        compiler_params=pltpu.CompilerParams(
            collective_id=0, has_side_effects=True, vmem_limit_bytes=48 * 1024 * 1024
        ),
        cost_estimate=pl.CostEstimate(flops=40 * 10**9, bytes_accessed=8 * 2**20, transcendentals=0),
    )(*(pltpu.with_memory_space_constraint(value, pltpu.HBM) for value in operands))
    return pl.pallas_call(
        store_kernel,
        out_shape=tuple(pltpu.HBM(value.shape, F32) for value in results),
        in_specs=[anywhere] * 3,
        out_specs=(anywhere,) * 3,
        scratch_shapes=[dma((3,))],
        cost_estimate=pl.CostEstimate(flops=0, bytes_accessed=4 * 2**20, transcendentals=0),
    )(*(pltpu.with_memory_space_constraint(value, pltpu.VMEM) for value in results))


def solution(mesh):
    specs = (P("tm", None, "row", None),) + (P("tm", "row"),) * 5
    return jax.shard_map(body, mesh=mesh, in_specs=specs, out_specs=specs[:3], check_vma=False)
```

```python
import functools
import math

import jax
import jax.numpy as jnp
from jax import lax
from jax.experimental import pallas as pl
from jax.experimental.pallas import tpu as pltpu
from jax.sharding import PartitionSpec as P

PUSH_GAIN = 0.5
PHASE_ADVANCE = 1.0
SOURCE_GAIN = 1.0
LANES = 512
BF16 = jnp.bfloat16
F32 = jnp.float32


def split(value):
    high = value.astype(BF16)
    return high, (value - high.astype(F32)).astype(BF16)


def sine_cosine(angle):
    count = jnp.round(angle * (2.0 / math.pi))
    rest = angle - count * 1.5703125
    rest = rest - count * 4.837512969970703125e-4
    rest = rest - count * 7.54978995489188216e-8
    quadrant = count.astype(jnp.int32)
    square = rest * rest
    sine = rest + rest * square * (
        -1.6666654611e-1 + square * (8.3321608736e-3 + square * -1.9515295891e-4)
    )
    cosine = 1.0 + square * (
        -0.5 + square * (4.166664568298827e-2 + square * (-1.388731625493765e-3 + square * 2.443315711809948e-5))
    )
    swapped = (quadrant & 1) == 1
    sine_out = jnp.where(swapped, cosine, sine)
    cosine_out = jnp.where(swapped, sine, cosine)
    sine_out = jnp.where((quadrant & 2) == 2, -sine_out, sine_out)
    cosine_out = jnp.where(((quadrant + 1) & 2) == 2, -cosine_out, cosine_out)
    return sine_out, cosine_out


def tiled(row, count):
    tile = jnp.broadcast_to(row, (16, row.shape[1])).astype(BF16)
    return jnp.concatenate([tile] * (count // 16), 0)


def fill_matrix(mat):
    length = mat.shape[2]
    away = lax.broadcasted_iota(jnp.int32, (length, length), 0) - lax.broadcasted_iota(jnp.int32, (length, length), 1)
    turn = lax.rem(away * away, 2 * length).astype(F32)
    sine, cosine = sine_cosine((math.pi / length) * turn - math.pi / 4)
    for number, value in enumerate((cosine, sine)):
        for part, piece in enumerate(split(value * (1.0 / math.sqrt(length)))):
            mat[part, pl.ds(number * length, length), :] = piece


def dot(left, right):
    return jnp.dot(left, right, preferred_element_type=F32)


def push(field, cell, hot, sampled):
    phase, energy, offset, row, col = (cell.at[item] for item in range(5))
    rows, cols = field.shape[1], field.shape[2]
    half_rows = rows // 2
    window = half_rows + 16
    groups = row.shape[0] // 2
    lanes = row.shape[1]
    cells = lax.broadcasted_iota(jnp.int32, (cols, lanes), 0).astype(F32).astype(BF16)
    one, zero = jnp.ones((cols, lanes), BF16), jnp.zeros((cols, lanes), BF16)
    for half in range(2):
        start = 0 if half == 0 else half_rows - 16
        parts = jnp.concatenate(split(field[:, pl.ds(start, window), :].reshape(2 * window, cols)), 1)
        row_ids = (lax.broadcasted_iota(jnp.int32, (window, lanes), 0) + start).astype(F32)
        for group in range(groups):
            at = half * groups + group
            here = pl.ds(at, 1)
            one_hot = jnp.where(cells == tiled(col[here, :], cols), one, zero)
            hot[:, pl.ds(at * lanes, lanes)] = one_hot
            mixed = dot(parts, jnp.concatenate([one_hot, one_hot], 0))
            place = row[here, :]
            f = offset[here, :]
            weight = jnp.where(row_ids == place - 1.0, 0.5 * (0.5 - f) * (0.5 - f), 0.0)
            weight = jnp.where(row_ids == place, 0.75 - f * f, weight)
            weight = jnp.where(row_ids == place + 1.0, 0.5 * (0.5 + f) * (0.5 + f), weight)
            sampled[0, here, :] = jnp.sum(weight * mixed[:window], axis=0, keepdims=True)
            sampled[1, here, :] = jnp.sum(weight * mixed[window:], axis=0, keepdims=True)
    sine, cosine = sine_cosine(phase[...])
    energy[...] = energy[...] - PUSH_GAIN * (sampled[0] * cosine - sampled[1] * sine)
    phase[...] = phase[...] + PHASE_ADVANCE * energy[...]


def deposit(field, cell, hot, source):
    phase, row = cell[0], cell.at[3]
    rows = field.shape[1]
    half_rows = rows // 2
    groups = row.shape[0] // 2
    lanes = row.shape[1]
    sine, cosine = sine_cosine(phase)
    source[0] = SOURCE_GAIN * cosine
    source[1] = -SOURCE_GAIN * sine
    one, zero = jnp.ones((half_rows, lanes), BF16), jnp.zeros((half_rows, lanes), BF16)
    for half in range(2):
        row_ids = (lax.broadcasted_iota(jnp.int32, (half_rows, lanes), 0) + half * half_rows).astype(F32).astype(BF16)
        spread = []
        for group in range(groups):
            here = pl.ds(half * groups + group, 1)
            match = jnp.where(row_ids == tiled(row[here, :], half_rows), one, zero)
            parts = []
            for part in range(2):
                value = source[part, here, :]
                high = value.astype(BF16).astype(F32)
                parts += [match * tiled(high, half_rows), match * tiled(value - high, half_rows)]
            spread.append(jnp.concatenate(parts, 0))
        total = lax.dot_general(
            jnp.concatenate(spread, 1),
            hot[:, pl.ds(half * groups * lanes, groups * lanes)],
            (((1,), (1,)), ((), ())),
            preferred_element_type=F32,
        )
        own = pl.ds(half * half_rows, half_rows)
        for part in range(2):
            first = total[2 * part * half_rows : (2 * part + 1) * half_rows]
            second = total[(2 * part + 1) * half_rows : (2 * part + 2) * half_rows]
            field[part, own, :] += first + second


def diffract(field, out, mat):
    rows, cols = field.shape[1], field.shape[2]
    mat_high, mat_low = mat[0], mat[1]
    wide_high = jnp.concatenate([mat_high[:cols], mat_high[cols:]], 1)
    wide_low = jnp.concatenate([mat_low[:cols], mat_low[cols:]], 1)
    wide = jnp.concatenate([wide_high, wide_high, wide_low], 0)
    high, low = split(field[...].reshape(2 * rows, cols))
    turned = dot(jnp.concatenate([high, low, high], 1), wide)
    real = turned[:rows, :cols] - turned[rows:, cols:]
    imag = turned[:rows, cols:] + turned[rows:, :cols]
    high, low = split(jnp.concatenate([real, imag], 1))
    turned = dot(jnp.concatenate([mat_high, mat_high, mat_low], 1), jnp.concatenate([high, low, high], 0))
    out[0] = turned[:rows, :cols] - turned[rows:, cols:]
    out[1] = turned[:rows, cols:] + turned[rows:, :cols]


def kernel(
    blocks, wave, phase_hbm, energy_hbm, offset_hbm, row_hbm, col_hbm,
    wave_out, phase_out, energy_out,
    field, cells, pack, packed, leave, arrive, hot, sampled, source,
    phase_in, energy_in, offset_in, row_in, col_in, mat, load_sem,
    near_sem, far_send, far_recv, part_send, part_recv, own_sem, hand_sem,
    out_send, out_recv, out_own, out_last, leave_send, leave_recv, leave_last,
):
    t, r = lax.axis_index("tm"), lax.axis_index("row")
    other = 1 - r
    p = lax.rem(r + t, 2)
    first_after = lax.rem(t + 1, 2)
    after, before = lax.rem(t + 1, blocks), lax.rem(t + blocks - 1, blocks)
    slots = field.shape[0]
    half_rows = field.shape[2] // 2
    groups = cells.shape[2] // 2
    lanes = cells.shape[3]
    mine, theirs = pl.ds(r * half_rows, half_rows), pl.ds(other * half_rows, half_rows)
    inputs = (phase_in, energy_in, offset_in, row_in, col_in)
    sources = (phase_hbm, energy_hbm, offset_hbm, row_hbm, col_hbm)
    loads = [
        pltpu.make_async_copy(src, dst, load_sem.at[number])
        for number, (src, dst) in enumerate(zip(sources, inputs))
    ]
    for load in loads:
        load.start()

    def remote(src, dst, send, recv, where):
        return pltpu.make_async_remote_copy(
            src_ref=src, dst_ref=dst, send_sem=send, recv_sem=recv,
            device_id=where, device_id_type=pl.DeviceIdType.MESH,
        )

    def send_half(slot):
        item = slots * (1 - p) + slot - 1
        return remote(wave.at[item], field.at[slot, :, mine, :], near_sem.at[0, slot], near_sem.at[1, slot], (t, other))

    def receive_half(slot):
        return remote(wave.at[0], field.at[slot, :, theirs, :], near_sem.at[0, slot], near_sem.at[1, slot], (t, other))

    def send_last(half):
        return remote(
            wave.at[wave.shape[0] - 1], field.at[0, :, pl.ds(half * half_rows, half_rows), :],
            far_send.at[0], far_recv.at[half], (after, first_after),
        )

    def own_half(slot):
        return pltpu.make_async_copy(wave.at[slots * p + slot - 1], field.at[slot, :, mine, :], own_sem.at[slot])

    def send_part(pair):
        return remote(pack.at[pair], packed.at[pair], part_send.at[pair], part_recv.at[pair], (t, other))

    def pack_pair(pair):
        for slot in range(2 * pair, 2 * pair + 2):
            for number, ref in enumerate(inputs):
                kept = ref[pl.ds(slots * p + slot, 1), :].astype(F32)
                sent = ref[pl.ds(slots * (1 - p) + slot, 1), :].astype(F32)
                base = ((slot % 2) * 5 + number) * groups
                for group in range(groups):
                    piece = slice(group * lanes, (group + 1) * lanes)
                    cells[slot, number, pl.ds(r * groups + group, 1), :] = kept[:, piece]
                    pack[pair, pl.ds(base + group, 1), :] = sent[:, piece]

    def hand_over():
        return remote(
            cells.at[0], cells.at[slots], hand_sem.at[0], hand_sem.at[1],
            (jnp.where(p == 1, t, before), jnp.where(p == 1, other, r)),
        )

    def is_last(slot):
        return (p == 1) & (slot == slots - 1)

    def goal(slot):
        last = is_last(slot)
        return jnp.where(last, after, t), jnp.where(last, 0, slots * p + slot + 1)

    def send_out(slot):
        block, item = goal(slot)
        return remote(
            field.at[slot, :, theirs, :], wave_out.at[item], out_send.at[slot], out_recv.at[item], (block, other)
        )

    def send_out_last():
        return remote(field.at[slots - 1, :, mine, :], wave_out.at[0], out_last.at[0], out_recv.at[0], (after, r))

    def own_out(slot):
        return pltpu.make_async_copy(
            field.at[slot, :, mine, :], wave_out.at[slots * p + slot + 1], out_own.at[slot]
        )

    def send_leave(slot):
        block, item = goal(slot)
        return remote(
            leave.at[slot, other], arrive.at[item], leave_send.at[slot], leave_recv.at[item], (block, other)
        )

    def send_leave_last():
        return remote(leave.at[slots - 1, r], arrive.at[0], leave_last.at[0], leave_recv.at[0], (after, r))

    barrier = pltpu.get_barrier_semaphore()
    for peer in ((t, other), (after, 0), (after, 1), (before, 0), (before, 1)):
        pl.semaphore_signal(barrier, inc=1, device_id=peer, device_id_type=pl.DeviceIdType.MESH)

    pl.semaphore_wait(barrier, 5)

    @pl.when(t < blocks - 1)
    def _():
        send_last(r).start()

    @pl.when(p == 0)
    def _():
        send_half(0).start()

    @pl.when(p == 1)
    def _():
        own_half(0).start()

    for load in loads:
        load.wait()
    pack_pair(0)
    send_part(0).start()
    for pair in range(1, slots // 2):
        pack_pair(pair)
    for slot in range(1, slots):
        own_half(slot).start()

    fill_matrix(mat)

    @pl.when((t == 0) & (p == 0))
    def _():
        field[0] = jnp.zeros(field.shape[1:], F32)

    @pl.loop(0, 2 * slots)
    def _(turn):
        ending = turn == 2 * slots - 2
        final = turn == 2 * slots - 1
        second = ((turn > 0) & (turn % 2 == 0)) | final
        slot = jnp.where(turn % 2 == 0, jnp.maximum(turn // 2 - 1, 0), (turn + 1) // 2)
        slot = jnp.where(ending, slots - 1, jnp.where(final, slots - 2, slot))
        cell = slot + second.astype(jnp.int32)

        @pl.when(turn == 0)
        def _():
            @pl.when(p == 0)
            def _():
                send_half(0).wait_send()

            @pl.when((p == 1) & (t < blocks - 1))
            def _():
                send_last(r).wait_send()

            send_half(1).start()

        @pl.when(jnp.logical_not(second))
        def _():
            pair, base = slot // 2, (slot % 2) * (5 * groups)

            @pl.when(slot % 2 == 0)
            def _():
                send_part(pair).wait_recv()

            for number in range(5):
                for group in range(groups):
                    cells[slot, number, pl.ds(other * groups + group, 1), :] = packed[
                        pair, pl.ds(base + number * groups + group, 1), :
                    ]

            @pl.when((p == 1) | (slot > 0))
            def _():
                own_half(slot).wait()
                receive_half(slot).wait_recv()

            @pl.when((p == 0) & (slot == 0) & (t > 0))
            def _():
                send_last(0).wait_recv()
                send_last(1).wait_recv()


        @pl.when(ending)
        def _():
            hand_over().wait_recv()

            @pl.when((p == 1) & (t == blocks - 1))
            def _():
                field[slots - 1] = jnp.zeros(field.shape[1:], F32)

        @pl.when(turn == 1)
        def _():
            for pair in range(1, slots // 2):
                send_part(pair).start()

        @pl.when((turn > 0) & (turn < slots - 1))
        def _():
            send_half(turn + 1).start()

        here = field.at[slot]
        push(here, cells.at[cell], hot, sampled)

        @pl.when(turn == 0)
        def _():
            hand_over().start()

        @pl.when(second)
        def _():
            for half in range(2):
                for number in range(2):
                    leave[slot, half, pl.ds(number * groups, groups), :] = cells[
                        cell, number, half * groups : (half + 1) * groups, :
                    ]
            send_leave(slot).start()

            @pl.when(is_last(slot))
            def _():
                send_leave_last().start()

            @pl.when(jnp.logical_not(is_last(slot)))
            def _():
                arrive[slots * p + slot + 1] = leave[slot, r]

        deposit(here, cells.at[cell], hot, source)

        diffract(here, here, mat)

        @pl.when(second)
        def _():
            send_out(slot).start()

            @pl.when(is_last(slot))
            def _():
                send_out_last().start()

            @pl.when(jnp.logical_not(is_last(slot)))
            def _():
                own_out(slot).start()

    def receive_leave(item):
        return remote(leave.at[0, 0], arrive.at[item], leave_send.at[0], leave_recv.at[item], (t, other))

    def receive_out(item):
        return remote(field.at[0, :, mine, :], wave_out.at[item], out_send.at[0], out_recv.at[item], (t, other))

    receive_leave(0).wait_recv()

    @pl.loop(0, slots)
    def _(slot):
        item = slots * (1 - p) + slot + 1

        @pl.when(item < 2 * slots)
        def _():
            receive_leave(item).wait_recv()

    for item in range(2 * slots):
        for group in range(groups):
            piece = pl.ds(group * lanes, lanes)
            phase_out[pl.ds(item, 1), piece] = arrive[item, pl.ds(group, 1), :]
            energy_out[pl.ds(item, 1), piece] = arrive[item, pl.ds(groups + group, 1), :]

    @pl.when((p == 0) & (t < blocks - 1))
    def _():
        send_last(r).wait_send()

    hand_over().wait_send()
    for pair in range(slots // 2):
        send_part(pair).wait_send()
    for slot in range(slots):
        if slot > 0:
            send_half(slot).wait_send()
        send_leave(slot).wait_send()
        send_out(slot).wait_send()

        @pl.when(is_last(slot))
        def _():
            send_leave_last().wait_send()
            send_out_last().wait_send()

        @pl.when(jnp.logical_not(is_last(slot)))
        def _():
            own_out(slot).wait()

    receive_out(0).wait_recv()

    @pl.loop(0, slots)
    def _(slot):
        item = slots * (1 - p) + slot + 1

        @pl.when(item < 2 * slots)
        def _():
            receive_out(item).wait_recv()


def store_kernel(*refs):
    sem = refs[-1]
    copies = [pltpu.make_async_copy(refs[i], refs[3 + i], sem.at[i]) for i in range(3)]
    for copy in copies:
        copy.start()
    for copy in copies:
        copy.wait()


def body(wavefront, particle_phase, particle_energy, row_offset, row_cell, col_cell):
    items, _, half_rows, cols = wavefront.shape
    slots, rows = items // 2, 2 * half_rows
    width = particle_phase.shape[1]
    groups = width // LANES
    operands = (wavefront, particle_phase, particle_energy, row_offset, row_cell, col_cell)
    vmem = pl.BlockSpec(memory_space=pltpu.VMEM)
    anywhere = pl.BlockSpec(memory_space=pl.ANY)
    dma = pltpu.SemaphoreType.DMA
    results = pl.pallas_call(
        functools.partial(kernel, lax.axis_size("tm")),
        out_shape=(
            pltpu.VMEM(wavefront.shape, F32),
            pltpu.VMEM(particle_phase.shape, F32),
            pltpu.VMEM(particle_phase.shape, F32),
        ),
        in_specs=[pl.BlockSpec(memory_space=pltpu.HBM)] * 6,
        out_specs=(anywhere, vmem, vmem),
        scratch_shapes=[
            pltpu.VMEM((slots, 2, rows, cols), F32),
            pltpu.VMEM((slots + 1, 5, 2 * groups, LANES), F32),
            pltpu.VMEM((slots // 2, 10 * groups, LANES), F32),
            pltpu.VMEM((slots // 2, 10 * groups, LANES), F32),
            pltpu.VMEM((slots, 2, 2 * groups, LANES), F32),
            pltpu.VMEM((items, 2 * groups, LANES), F32),
            pltpu.VMEM((cols, 2 * width), BF16),
            pltpu.VMEM((2, 2 * groups, LANES), F32),
            pltpu.VMEM((2, 2 * groups, LANES), F32),
            *[pltpu.VMEM(particle_phase.shape, F32)] * 3,
            *[pltpu.VMEM(particle_phase.shape, jnp.int32)] * 2,
            pltpu.VMEM((2, 2 * cols, cols), BF16),
            dma((5,)),
            dma((2, slots)), dma((1,)), dma((2,)), dma((slots // 2,)), dma((slots // 2,)), dma((slots,)), dma((2,)),
            dma((slots,)), dma((items,)), dma((slots,)), dma((1,)), dma((slots,)), dma((items,)), dma((1,)),
        ],
        compiler_params=pltpu.CompilerParams(
            collective_id=0, has_side_effects=True, vmem_limit_bytes=48 * 1024 * 1024
        ),
        cost_estimate=pl.CostEstimate(flops=40 * 10**9, bytes_accessed=8 * 2**20, transcendentals=0),
    )(*(pltpu.with_memory_space_constraint(value, pltpu.HBM) for value in operands))
    return pl.pallas_call(
        store_kernel,
        out_shape=tuple(pltpu.HBM(value.shape, F32) for value in results),
        in_specs=[anywhere] * 3,
        out_specs=(anywhere,) * 3,
        scratch_shapes=[dma((3,))],
        cost_estimate=pl.CostEstimate(flops=0, bytes_accessed=4 * 2**20, transcendentals=0),
    )(*(pltpu.with_memory_space_constraint(value, pltpu.VMEM) for value in results))


def solution(mesh):
    specs = (P("tm", None, "row", None),) + (P("tm", "row"),) * 5
    return jax.shard_map(body, mesh=mesh, in_specs=specs, out_specs=specs[:3], check_vma=False)
```
